128 devices in a mesh: wide: 32 (over z, y, core), narrow: 4 (over x).
Axes of the slice: x: 4, y: 4, z: 4, core: 2. Of those that a mesh axis runs over, the one named last changes fastest.
Arguments:
- inputs: bfloat16 [256, 32768], P('narrow', 'wide'), may hold values from -6 to 6
- out_grad: bfloat16 [256, 32768], P('narrow', 'wide'), may hold values from -6 to 6
- residues: float32 [256, 16], P('narrow'), may hold values from -4 to 4
- decay: float32 [256, 16], P('narrow'), may hold values from 1e-05 to 0.05
Outputs:
- filter_grad: float32 [256, 32768], P('narrow', 'wide')
- residue_grad: float32 [256, 16], P('narrow')
- log_decay_grad: float32 [256, 16], P('narrow')
The draws below stay inside these ranges and needn't reach their ends.
All inputs are finite; a program needn't handle non-finite values.
Results may differ from the reference program's by a relative error of at most 0.0003.
Values may be sent and summed in bfloat16 or wider, within the bound.
A program may use at most 64 MiB of HBM per device.

```python
import math
import jax
import jax.numpy as jnp
from jax import lax

CHANNELS = 256
ORDER = 16
SEQ = 32768


def block_levels(own_key, dims, shards, least, top_value):
    def one(axis_at, shards_of):
        steps = jax.random.uniform(jax.random.fold_in(jax.random.fold_in(own_key, 6), axis_at), (shards_of,), jnp.float32, least / len(shards), top_value / len(shards))
        return jnp.repeat(jnp.exp(steps), dims[axis_at] // shards_of).reshape((-1,) + (1,) * (len(dims) - axis_at - 1))

    factor_of = one(*shards[0])
    for cut in shards[1:]:
        factor_of = factor_of * one(*cut)
    return factor_of


def noise(stream_key, shape, width, bound, pieces=(), kind=jnp.bfloat16):
    level = block_levels(stream_key, shape, pieces, -0.22, 0.18) if pieces else 1.0
    result = jax.random.normal(stream_key, shape, jnp.float32) * width * level
    return jnp.minimum(jnp.maximum(result, -bound), bound).astype(kind)


def setup_inputs(seed: int = 0) -> dict:
    key_of = jax.random.split(jax.random.key(seed), 5)
    inputs = noise(key_of[0], (CHANNELS, SEQ), 1.0, 6.0, ((0, 4), (1, 32)))
    out_grad = noise(key_of[1], (CHANNELS, SEQ), 1.0, 6.0, ((0, 4), (1, 32)))
    residues = noise(key_of[2], (CHANNELS, ORDER), 1.0, 4.0, ((0, 4),), jnp.float32)
    decay = jnp.clip(jnp.exp(math.log(0.05) - 8.517193 * jax.random.uniform(key_of[3], (CHANNELS, ORDER), jnp.float32) ** block_levels(key_of[3], (CHANNELS, ORDER), ((0, 4),), -0.2, 0.2)), 9.999999747378752e-06, 0.05)
    return dict(inputs=inputs, out_grad=out_grad, residues=residues, decay=decay)


def reference(inputs, out_grad, residues, decay):
    length = inputs.shape[1]
    scale = 1.0 / jnp.sqrt(jnp.float32(length))
    signal = inputs.astype(jnp.float32)
    grad_out = out_grad.astype(jnp.float32)
    spec_in = jnp.fft.rfft(signal, n=2 * length, axis=1)
    spec_out = jnp.fft.rfft(grad_out, n=2 * length, axis=1)
    corr = jnp.fft.irfft(spec_out * jnp.conj(spec_in), n=2 * length, axis=1)[:, :length]
    filter_grad = (scale * corr).astype(jnp.float32)
    lags = jnp.arange(length).astype(jnp.float32)

    def one_channel(packed):
        taps, rates = packed
        power = jnp.exp(-rates[:, None] * lags[None, :])
        first = jnp.dot(power, taps, precision=lax.Precision.HIGHEST)
        second = jnp.dot(power, taps * lags, precision=lax.Precision.HIGHEST)
        return (first, second)
    first, second = lax.map(one_channel, (filter_grad, decay))
    residue_grad = scale * first
    log_decay_grad = -scale * decay * residues * second
    return (filter_grad, residue_grad, log_decay_grad)
```

```python
import math

import jax
import jax.numpy as jnp
from jax import lax
from jax.experimental import pallas as pl
from jax.experimental.pallas import tpu as pltpu
from jax.sharding import PartitionSpec as P

F32 = jnp.float32
BF16 = jnp.bfloat16
MESH = pl.DeviceIdType.MESH

LANES = 128
SHIFTS = 32
TURNS = LANES // SHIFTS


def to_rows(block_ref, stage, send):
    chans, width = block_ref.shape
    tiles = width // LANES
    for k in range(tiles):
        stage[pl.ds(k, chans, stride=tiles), :] = block_ref[:, k * LANES : (k + 1) * LANES].astype(F32)
    send[...] = stage[...].astype(BF16)


def build_toeplitz(ch, signal, toep):
    row = lax.broadcasted_iota(jnp.int32, (SHIFTS, LANES), 0)
    lane = lax.broadcasted_iota(jnp.int32, (SHIFTS, LANES), 1)
    keep = lane >= row

    def step(i, before):
        for p in range(2):
            for q in range(8):
                m = 16 * i + 8 * p + q
                spread = jnp.broadcast_to(signal[ch, pl.ds(m, 1), :], (SHIFTS, LANES))
                now = pltpu.roll(spread, 0, 1, stride=1, stride_axis=0)
                toep[ch, i, q * SHIFTS : (q + 1) * SHIFTS, p * LANES : (p + 1) * LANES] = jnp.where(
                    keep, now, before
                ).astype(BF16)
                before = now
        return before

    lax.fori_loop(0, 16, step, jnp.zeros((SHIFTS, LANES), F32))


def build_shifted(ch, grad, shifted):
    lane = lax.broadcasted_iota(jnp.int32, (264, LANES), 1)
    here = grad[ch, 0:264, :]
    after = grad[ch, 1:265, :]
    for h in range(TURNS):
        moved = here
        if h:
            moved = pltpu.roll(jnp.where(lane < SHIFTS * h, after, here), LANES - SHIFTS * h, 1)
        shifted[ch, h] = jnp.concatenate([moved[0:256], moved[8:264]], axis=1).astype(BF16)


def correlate(ch, toep, shifted, acc, scale):
    acc[...] = jnp.zeros_like(acc)
    for i in range(16):
        live = 256 - 16 * i
        table = toep[ch, i]
        for h in range(TURNS):
            part = lax.dot_general(
                shifted[ch, h, 16 * i : 256, :],
                table,
                (((1,), (1,)), ((), ())),
                preferred_element_type=F32,
            )
            acc[h, 0, 0:live] += part[:, :LANES]
            acc[h, 1, 0:live] += part[:, LANES:]
    group = lax.broadcasted_iota(jnp.int32, (256, LANES), 1) // SHIFTS
    total = None
    for turn in range(TURNS):
        mixed = None
        for low in range(TURNS):
            h = (low + turn) % TURNS
            term = acc[h, 0, low : low + 256, :] + acc[h, 1, low + 4 : low + 260, :]
            mixed = term if mixed is None else jnp.where(group == low, term, mixed)
        if turn:
            mixed = pltpu.roll(mixed, SHIFTS * turn, 1)
        total = mixed if total is None else total + mixed
    return total * scale


def kernel(
    x_ref, g_ref, res_ref, dec_ref, out_ref, rg_ref, ld_ref,
    stage, send_x, send_g, recv_x, recv_g, signal, grad, toep, shifted, acc,
    send_c, recv_c, fine, coarse, send_m, recv_m,
    ssem_in, rsem_in, ssem_c, rsem_c, ssem_m, rsem_m,
):
    count = lax.axis_size("wide")
    me = lax.axis_index("wide")
    seq = count * x_ref.shape[1]
    scale = 1.0 / math.sqrt(seq)

    barrier = pltpu.get_barrier_semaphore()

    @pl.loop(1, count)
    def _(k):
        pl.semaphore_signal(
            barrier, inc=1, device_id={"wide": lax.rem(me + k, count)}, device_id_type=MESH
        )

    to_rows(x_ref, stage, send_x)
    to_rows(g_ref, stage, send_g)
    pl.semaphore_wait(barrier, count - 1)

    def moved(which, send, recv, to, at):
        return pltpu.make_async_remote_copy(
            src_ref=send.at[pl.ds(pl.multiple_of(16 * to, 16), 16), :],
            dst_ref=recv.at[pl.ds(pl.multiple_of(16 * at, 16), 16), :],
            send_sem=ssem_in.at[which, to],
            recv_sem=rsem_in.at[which, at],
            device_id={"wide": to},
            device_id_type=MESH,
        )

    @pl.loop(1, count)
    def _(k):
        moved(0, send_x, recv_x, lax.rem(me + k, count), me).start()

    @pl.loop(1, count)
    def _(k):
        moved(1, send_g, recv_g, lax.rem(me + k, count), me).start()

    mine = pl.ds(pl.multiple_of(16 * me, 16), 16)
    recv_x[mine, :] = send_x[mine, :]
    recv_g[mine, :] = send_g[mine, :]

    lane_big = lax.broadcasted_iota(jnp.int32, (256, LANES), 1)
    block_at = (lax.broadcasted_iota(jnp.int32, (256, LANES), 0) * LANES).astype(F32)
    lane_small = lax.broadcasted_iota(jnp.int32, (LANES, LANES), 1)
    offset_at = lax.broadcasted_iota(jnp.int32, (LANES, LANES), 0).astype(F32)
    rates = []
    for ch in range(2):
        rate = dec_ref[pl.ds(2 * me + ch, 1), :]
        rate = jnp.concatenate([rate] * 8, axis=1)
        rates.append(rate)
        power = jnp.exp(-rate * offset_at)
        weighted = jnp.logical_and(lane_small >= 16, lane_small < 32)
        fine[ch] = jnp.where(lane_small < 48, jnp.where(weighted, offset_at * power, power), 0.0)
        power = jnp.exp(-rate * block_at)
        coarse[ch] = jnp.where(lane_big < 32, power, block_at * power)

    @pl.loop(1, count)
    def _(k):
        at = lax.rem(me + k, count)
        moved(0, send_x, recv_x, at, at).wait_recv()

    wide = recv_x[...].astype(F32).reshape(32, 16, LANES)
    for ch in range(2):
        signal[ch] = wide[:, 8 * ch : 8 * ch + 8].reshape(256, LANES)
    for ch in range(2):
        build_toeplitz(ch, signal, toep)

    @pl.loop(1, count)
    def _(k):
        at = lax.rem(me + k, count)
        moved(1, send_g, recv_g, at, at).wait_recv()

    wide = recv_g[...].astype(F32).reshape(32, 16, LANES)
    for ch in range(2):
        grad[ch, 0:256] = wide[:, 8 * ch : 8 * ch + 8].reshape(256, LANES)
        grad[ch, 256:] = jnp.zeros((16, LANES), F32)
        build_shifted(ch, grad, shifted)

    def lags_to(ch, to, at):
        return pltpu.make_async_remote_copy(
            src_ref=send_c.at[ch, pl.ds(pl.multiple_of(8 * to, 8), 8), :],
            dst_ref=recv_c.at[pl.ds(pl.multiple_of(16 * at + 8 * ch, 8), 8), :],
            send_sem=ssem_c.at[ch, to],
            recv_sem=rsem_c.at[ch, at],
            device_id={"wide": to},
            device_id_type=MESH,
        )

    for ch in range(2):
        send_c[ch] = correlate(ch, toep, shifted, acc, scale)

        @pl.loop(1, count)
        def _(k):
            lags_to(ch, lax.rem(me + k, count), me).start()

        recv_c[pl.ds(pl.multiple_of(16 * me + 8 * ch, 8), 8), :] = send_c[
            ch, pl.ds(pl.multiple_of(8 * me, 8), 8), :
        ]

    lane_row = lax.broadcasted_iota(jnp.int32, (1, LANES), 1)
    sub = lax.broadcasted_iota(jnp.int32, (8, LANES), 0)
    tile = jnp.zeros((8, LANES), F32)
    for ch in range(2):
        part = jnp.dot(
            send_c[ch], fine[ch], precision=lax.Precision.HIGHEST, preferred_element_type=F32
        )
        sums = jnp.sum(part * coarse[ch], axis=0, keepdims=True)
        both = sums + pltpu.roll(sums, LANES - 16, 1)
        residue = jnp.concatenate([res_ref[pl.ds(2 * me + ch, 1), :]] * 8, axis=1)
        line = jnp.where(lane_row < 16, scale * sums, -scale * rates[ch] * residue * both)
        tile = tile + jnp.where(sub == 2 * lax.rem(me, 4) + ch, line, 0.0)
    send_m[...] = tile
    own = pl.ds(pl.multiple_of(8 * me, 8), 8)
    recv_m[own, :] = tile

    def modes_to(to, at):
        return pltpu.make_async_remote_copy(
            src_ref=send_m,
            dst_ref=recv_m.at[pl.ds(pl.multiple_of(8 * at, 8), 8), :],
            send_sem=ssem_m.at[to],
            recv_sem=rsem_m.at[at],
            device_id={"wide": to},
            device_id_type=MESH,
        )

    @pl.loop(1, count)
    def _(k):
        modes_to(lax.rem(me + k, count), me).start()

    @pl.loop(1, count)
    def _(k):
        at = lax.rem(me + k, count)
        for ch in range(2):
            lags_to(ch, at, at).wait_recv()

    chans = out_ref.shape[0]
    for k in range(8):
        out_ref[:, k * LANES : (k + 1) * LANES] = recv_c[pl.ds(k, chans, stride=8), :]

    @pl.loop(1, count)
    def _(k):
        at = lax.rem(me + k, count)
        modes_to(at, at).wait_recv()

    tiles = recv_m[...].reshape(8, 4, 8, LANES)
    rows = (tiles[:, 0] + tiles[:, 1] + tiles[:, 2] + tiles[:, 3]).reshape(64, LANES)
    rg_ref[...] = rows[:, 0:16]
    ld_ref[...] = rows[:, 16:32]

    @pl.loop(1, count)
    def _(k):
        to = lax.rem(me + k, count)
        moved(0, send_x, recv_x, to, me).wait_send()
        moved(1, send_g, recv_g, to, me).wait_send()
        for ch in range(2):
            lags_to(ch, to, me).wait_send()
        modes_to(to, me).wait_send()


def local(inputs, out_grad, residues, decay):
    chans, block = inputs.shape
    count = lax.axis_size("wide")
    vmem = pl.BlockSpec(memory_space=pltpu.VMEM)
    dma = pltpu.SemaphoreType.DMA
    return pl.pallas_call(
        kernel,
        out_shape=(
            jax.ShapeDtypeStruct((chans, block), F32),
            jax.ShapeDtypeStruct(residues.shape, F32),
            jax.ShapeDtypeStruct(decay.shape, F32),
        ),
        in_specs=[vmem] * 4,
        out_specs=(vmem,) * 3,
        scratch_shapes=[
            pltpu.VMEM((512, LANES), F32),
            pltpu.VMEM((512, LANES), BF16),
            pltpu.VMEM((512, LANES), BF16),
            pltpu.VMEM((512, LANES), BF16),
            pltpu.VMEM((512, LANES), BF16),
            pltpu.VMEM((2, 256, LANES), F32),
            pltpu.VMEM((2, 272, LANES), F32),
            pltpu.VMEM((2, 16, 256, 256), BF16),
            pltpu.VMEM((2, TURNS, 256, 256), BF16),
            pltpu.VMEM((TURNS, 2, 264, LANES), F32),
            pltpu.VMEM((2, 256, LANES), F32),
            pltpu.VMEM((512, LANES), F32),
            pltpu.VMEM((2, LANES, LANES), F32),
            pltpu.VMEM((2, 256, LANES), F32),
            pltpu.VMEM((8, LANES), F32),
            pltpu.VMEM((256, LANES), F32),
            dma((2, count)),
            dma((2, count)),
            dma((2, count)),
            dma((2, count)),
            dma((count,)),
            dma((count,)),
        ],
        compiler_params=pltpu.CompilerParams(
            collective_id=0, has_side_effects=True, vmem_limit_bytes=32 * 2**20
        ),
    )(inputs, out_grad, residues, decay)


def solution(mesh):
    placed = (P("narrow", "wide"), P("narrow", "wide"), P("narrow", None), P("narrow", None))
    return jax.shard_map(
        local,
        mesh=mesh,
        in_specs=placed,
        out_specs=(P("narrow", "wide"), P("narrow", None), P("narrow", None)),
        check_vma=False,
    )
```

```python
import math

import jax
import jax.numpy as jnp
from jax import lax
from jax.experimental import pallas as pl
from jax.experimental.pallas import tpu as pltpu
from jax.sharding import PartitionSpec as P

F32 = jnp.float32
BF16 = jnp.bfloat16
MESH = pl.DeviceIdType.MESH

LANES = 128
SHIFTS = 32
TURNS = LANES // SHIFTS
PEERS = 32
RING = (0, 1, 2, 1)
OFFSETS = sorted(
    ((dz, dy, dc) for dz in range(4) for dy in range(4) for dc in range(2) if dz or dy or dc),
    key=lambda o: (-RING[o[0]] - RING[o[1]], -o[2], o),
)


def place(me):
    return me // 8, (me // 2) % 4, me % 2


def shifted_peer(at, dz, dy, dc):
    z, y, core = at
    return ((z + dz) % 4) * 8 + ((y + dy) % 4) * 2 + (core + dc) % 2


def aligned(index, size):
    return pl.ds(pl.multiple_of(index * size, size), size)


def to_rows(block_ref, which, stage):
    for ch in range(2):
        for k in range(8):
            stage[pl.ds(16 * which + 8 * ch + k, PEERS, stride=32), :] = block_ref[
                PEERS * ch : PEERS * (ch + 1), k * LANES : (k + 1) * LANES
            ].astype(F32)


def build_toeplitz(j, recv, toep, tails):
    row = lax.broadcasted_iota(jnp.int32, (SHIFTS, LANES), 0)
    lane = lax.broadcasted_iota(jnp.int32, (SHIFTS, LANES), 1)
    keep = lane >= row
    block = recv[pl.ds(pl.multiple_of(32 * j, 32), 16), :].astype(F32)
    for ch in range(2):
        before = jnp.zeros((SHIFTS, LANES), F32)
        for q in range(8):
            spread = jnp.broadcast_to(block[8 * ch + q : 8 * ch + q + 1], (SHIFTS, LANES))
            now = pltpu.roll(spread, 0, 1, stride=1, stride_axis=0)
            toep[ch, j, q * SHIFTS : (q + 1) * SHIFTS, :] = jnp.where(keep, now, before).astype(BF16)
            before = now
        tails[ch, j] = jnp.where(keep, 0.0, before).astype(BF16)


def build_shifted(ch, grad, shifted):
    lane = lax.broadcasted_iota(jnp.int32, (264, LANES), 1)
    here = grad[ch, 0:264, :]
    after = grad[ch, 1:265, :]
    turns = []
    for h in range(TURNS):
        moved = here
        if h:
            moved = pltpu.roll(jnp.where(lane < SHIFTS * h, after, here), LANES - SHIFTS * h, 1)
        turns.append(jnp.concatenate([moved[0:256], moved[8:264]], axis=1).reshape(32, 8, 256))
    shifted[ch] = jnp.stack(turns, axis=1).reshape(1024, 256).astype(BF16)


def correlate(ch, toep, shifted, acc, scale):
    acc[...] = jnp.zeros_like(acc)
    for i in range(16):
        live = 256 - 16 * i
        table = jnp.concatenate([toep[ch, 2 * i], toep[ch, 2 * i + 1]], axis=1)
        part = lax.dot_general(
            shifted[ch, 64 * i : 1024, :],
            table,
            (((1,), (1,)), ((), ())),
            preferred_element_type=F32,
        ).reshape(live // 8, TURNS, 8, 256)
        for h in range(TURNS):
            own = part[:, h].reshape(live, 256)
            acc[h, 0, 0:live] += own[:, :LANES]
            acc[h, 1, 0:live] += own[:, LANES:]
    group = lax.broadcasted_iota(jnp.int32, (256, LANES), 1) // SHIFTS
    total = None
    for turn in range(TURNS):
        mixed = None
        for low in range(TURNS):
            h = (low + turn) % TURNS
            term = acc[h, 0, low : low + 256, :] + acc[h, 1, low + 4 : low + 260, :]
            mixed = term if mixed is None else jnp.where(group == low, term, mixed)
        if turn:
            mixed = pltpu.roll(mixed, SHIFTS * turn, 1)
        total = mixed if total is None else total + mixed
    return total * scale


def channel_row(ref, channel):
    lane = lax.broadcasted_iota(jnp.int32, ref.shape, 1)
    column = jnp.sum(jnp.where(lane == channel, ref[...], 0.0), axis=1, keepdims=True)
    spread = jnp.broadcast_to(column, (16, LANES))
    sub = lax.broadcasted_iota(jnp.int32, (16, LANES), 0)
    lane = lax.broadcasted_iota(jnp.int32, (16, LANES), 1)
    return jnp.sum(jnp.where(lane % 16 == sub, spread, 0.0), axis=0, keepdims=True)


def exchange(
    x_hbm, g_hbm, res_hbm, dec_hbm, recv_c, recv_m,
    x_ref, g_ref, res_ref, dec_ref, stage, send, recv, grad, toep, tails, shifted, acc,
    send_c, fine, coarse, send_m,
    lsem, ssem_in, rsem_in, ssem_c, rsem_c, ssem_m, rsem_m,
):
    me = lax.axis_index("wide")
    at = place(me)
    peers = [shifted_peer(at, *offset) for offset in OFFSETS]
    scale = 1.0 / math.sqrt(PEERS * x_ref.shape[1])

    barrier = pltpu.get_barrier_semaphore()
    for peer in peers:
        pl.semaphore_signal(barrier, inc=1, device_id={"wide": peer}, device_id_type=MESH)

    fetches = [
        pltpu.make_async_copy(src, dst, lsem.at[n])
        for n, (src, dst) in enumerate(
            ((x_hbm, x_ref), (g_hbm, g_ref), (dec_hbm, dec_ref), (res_hbm, res_ref))
        )
    ]
    for fetch in fetches:
        fetch.start()
    for which, ref in ((0, x_ref), (1, g_ref)):
        fetches[which].wait()
        to_rows(ref, which, stage)
    send[...] = stage[...].astype(BF16)
    pl.semaphore_wait(barrier, PEERS - 1)

    def signals_to(to, source):
        return pltpu.make_async_remote_copy(
            src_ref=send.at[aligned(to, 32), :],
            dst_ref=recv.at[aligned(source, 32), :],
            send_sem=ssem_in.at[to],
            recv_sem=rsem_in.at[source],
            device_id={"wide": to},
            device_id_type=MESH,
        )

    for peer in peers:
        signals_to(peer, me).start()
    recv[aligned(me, 32), :] = send[aligned(me, 32), :]

    fetches[2].wait()
    fetches[3].wait()
    lane_big = lax.broadcasted_iota(jnp.int32, (256, LANES), 1)
    block_at = (lax.broadcasted_iota(jnp.int32, (256, LANES), 0) * LANES).astype(F32)
    lane_small = lax.broadcasted_iota(jnp.int32, (LANES, LANES), 1)
    offset_at = lax.broadcasted_iota(jnp.int32, (LANES, LANES), 0).astype(F32)
    rates = []
    for ch in range(2):
        rate = channel_row(dec_ref, PEERS * ch + me)
        rates.append(rate)
        power = jnp.exp(-rate * offset_at)
        weighted = jnp.logical_and(lane_small >= 16, lane_small < 32)
        fine[ch] = jnp.where(lane_small < 48, jnp.where(weighted, offset_at * power, power), 0.0)
        power = jnp.exp(-rate * block_at)
        coarse[ch] = jnp.where(lane_big < 32, power, block_at * power)

    build_toeplitz(me, recv, toep, tails)

    def arrival(n, carry):
        dy, dz = (n // 2) % 4, n // 8
        dy = dy + (dy // 2) * (1 - 2 * (dy % 2))
        dz = dz + (dz // 2) * (1 - 2 * (dz % 2))
        source = shifted_peer(at, dz, dy, n % 2)
        signals_to(source, source).wait_recv()
        build_toeplitz(source, recv, toep, tails)
        return carry

    lax.fori_loop(1, PEERS, arrival, 0)

    for ch in range(2):
        toep[ch, 1:, 0:SHIFTS, :] = toep[ch, 1:, 0:SHIFTS, :] + tails[ch, : PEERS - 1]
        grad[ch, 0:256] = (
            recv[...].reshape(PEERS, 32, LANES)[:, 16:32].astype(F32)[:, 8 * ch : 8 * ch + 8]
        ).reshape(256, LANES)
        grad[ch, 256:] = jnp.zeros((16, LANES), F32)
        build_shifted(ch, grad, shifted)

    def lags_to(ch, to, source):
        return pltpu.make_async_remote_copy(
            src_ref=send_c.at[ch, aligned(to, 8), :],
            dst_ref=recv_c.at[pl.ds(pl.multiple_of(16 * source + 8 * ch, 8), 8), :],
            send_sem=ssem_c.at[ch, to],
            recv_sem=rsem_c.at[ch, source],
            device_id={"wide": to},
            device_id_type=MESH,
        )

    def modal(ch):
        part = jnp.dot(
            send_c[ch], fine[ch], precision=lax.Precision.HIGHEST, preferred_element_type=F32
        )
        sums = jnp.sum(part * coarse[ch], axis=0, keepdims=True)
        both = sums + pltpu.roll(sums, LANES - 16, 1)
        residue = channel_row(res_ref, PEERS * ch + me)
        lane = lax.broadcasted_iota(jnp.int32, (1, LANES), 1)
        line = jnp.where(lane < 16, scale * sums, -scale * rates[ch] * residue * both)
        return jnp.where(lane < 32, line, 0.0)

    lines = []
    for ch in range(2):
        send_c[ch] = correlate(ch, toep, shifted, acc, scale)
        for peer in peers:
            lags_to(ch, peer, me).start()
        recv_c[pl.ds(pl.multiple_of(16 * me + 8 * ch, 8), 8), :] = send_c[ch, aligned(me, 8), :]
        lines.append(modal(ch))
    line = lines[0] + pltpu.roll(lines[1], 32, 1)
    send_m[...] = line
    recv_m[me] = line

    def modes_to(to, source):
        return pltpu.make_async_remote_copy(
            src_ref=send_m,
            dst_ref=recv_m.at[source],
            send_sem=ssem_m.at[to],
            recv_sem=rsem_m.at[source],
            device_id={"wide": to},
            device_id_type=MESH,
        )

    for peer in peers:
        modes_to(peer, me).start()

    @pl.loop(1, PEERS)
    def _(k):
        peer = (me + k) % PEERS
        signals_to(peer, me).wait_send()
        lags_to(0, peer, me).wait_send()
        lags_to(1, peer, me).wait_send()
        modes_to(peer, me).wait_send()
        lags_to(0, peer, peer).wait_recv()
        lags_to(1, peer, peer).wait_recv()
        modes_to(peer, peer).wait_recv()


def regroup(c_ref, m_ref, out_ref, rg_ref, ld_ref):
    for ch in range(2):
        for k in range(8):
            out_ref[PEERS * ch : PEERS * (ch + 1), k * LANES : (k + 1) * LANES] = c_ref[
                pl.ds(8 * ch + k, PEERS, stride=16), :
            ]
    lines = jnp.transpose(m_ref[:, 0, :])
    rg_ref[...] = jnp.concatenate([lines[0:16], lines[32:48]], axis=1)
    ld_ref[...] = jnp.concatenate([lines[16:32], lines[48:64]], axis=1)


def local(inputs, out_grad, residues, decay):
    chans, block = inputs.shape
    modes = residues.shape[1]
    vmem = pl.BlockSpec(memory_space=pltpu.VMEM)
    hbm = pl.BlockSpec(memory_space=pltpu.HBM)
    dma = pltpu.SemaphoreType.DMA
    lags, lines = pl.pallas_call(
        exchange,
        out_shape=(
            jax.ShapeDtypeStruct((512, LANES), F32),
            jax.ShapeDtypeStruct((PEERS, 1, LANES), F32),
        ),
        in_specs=[hbm] * 4,
        out_specs=(vmem, vmem),
        scratch_shapes=[
            pltpu.VMEM((chans, block), BF16),
            pltpu.VMEM((chans, block), BF16),
            pltpu.VMEM((modes, chans), F32),
            pltpu.VMEM((modes, chans), F32),
            pltpu.VMEM((1024, LANES), F32),
            pltpu.VMEM((1024, LANES), BF16),
            pltpu.VMEM((1024, LANES), BF16),
            pltpu.VMEM((2, 272, LANES), F32),
            pltpu.VMEM((2, PEERS, 256, LANES), BF16),
            pltpu.VMEM((2, PEERS, SHIFTS, LANES), BF16),
            pltpu.VMEM((2, 1024, 256), BF16),
            pltpu.VMEM((TURNS, 2, 264, LANES), F32),
            pltpu.VMEM((2, 256, LANES), F32),
            pltpu.VMEM((2, LANES, LANES), F32),
            pltpu.VMEM((2, 256, LANES), F32),
            pltpu.VMEM((1, LANES), F32),
            dma((4,)),
            dma((PEERS,)),
            dma((PEERS,)),
            dma((2, PEERS)),
            dma((2, PEERS)),
            dma((PEERS,)),
            dma((PEERS,)),
        ],
        compiler_params=pltpu.CompilerParams(
            collective_id=0, has_side_effects=True, vmem_limit_bytes=32 * 2**20
        ),
    )(inputs, out_grad, residues.T, decay.T)
    filter_grad, residue_grad, log_decay_grad = pl.pallas_call(
        regroup,
        out_shape=(
            jax.ShapeDtypeStruct((chans, block), F32),
            jax.ShapeDtypeStruct((modes, chans), F32),
            jax.ShapeDtypeStruct((modes, chans), F32),
        ),
        in_specs=[vmem] * 2,
        out_specs=(vmem,) * 3,
    )(lags, lines)
    return filter_grad, residue_grad.T, log_decay_grad.T


def solution(mesh):
    placed = (P("narrow", "wide"), P("narrow", "wide"), P("narrow", None), P("narrow", None))
    return jax.shard_map(
        local,
        mesh=mesh,
        in_specs=placed,
        out_specs=(P("narrow", "wide"), P("narrow", None), P("narrow", None)),
        check_vma=False,
    )
```

```python
import math

import jax
import jax.numpy as jnp
from jax import lax
from jax.experimental import pallas as pl
from jax.experimental.pallas import tpu as pltpu
from jax.sharding import PartitionSpec as P

F32 = jnp.float32
BF16 = jnp.bfloat16
MESH = pl.DeviceIdType.MESH

LANES = 128
SHIFTS = 32
TURNS = LANES // SHIFTS
PEERS = 32
RING = (0, 1, 2, 1)
OFFSETS = sorted(
    ((dz, dy, dc) for dz in range(4) for dy in range(4) for dc in range(2) if dz or dy or dc),
    key=lambda o: (-RING[o[0]] - RING[o[1]], -o[2], o),
)


def place(me):
    return me // 8, (me // 2) % 4, me % 2


def shifted_peer(at, dz, dy, dc):
    z, y, core = at
    return ((z + dz) % 4) * 8 + ((y + dy) % 4) * 2 + (core + dc) % 2


def aligned(index, size):
    return pl.ds(pl.multiple_of(index * size, size), size)


def to_rows(block_ref, stage, send):
    for ch in range(2):
        for k in range(8):
            stage[pl.ds(8 * ch + k, PEERS, stride=16), :] = block_ref[
                PEERS * ch : PEERS * (ch + 1), k * LANES : (k + 1) * LANES
            ].astype(F32)
    send[...] = stage[...].astype(BF16)


def build_toeplitz(j, recv, toep, tails):
    row = lax.broadcasted_iota(jnp.int32, (SHIFTS, LANES), 0)
    lane = lax.broadcasted_iota(jnp.int32, (SHIFTS, LANES), 1)
    keep = lane >= row
    block = recv[aligned(j, 16), :].astype(F32)
    for ch in range(2):
        before = jnp.zeros((SHIFTS, LANES), F32)
        for q in range(8):
            spread = jnp.broadcast_to(block[8 * ch + q : 8 * ch + q + 1], (SHIFTS, LANES))
            now = pltpu.roll(spread, 0, 1, stride=1, stride_axis=0)
            toep[ch, j, q * SHIFTS : (q + 1) * SHIFTS, :] = jnp.where(keep, now, before).astype(BF16)
            before = now
        tails[ch, j] = jnp.where(keep, 0.0, before).astype(BF16)


def build_shifted(ch, grad, shifted):
    lane = lax.broadcasted_iota(jnp.int32, (264, LANES), 1)
    here = grad[ch, 0:264, :]
    after = grad[ch, 1:265, :]
    turns = []
    for h in range(TURNS):
        moved = here
        if h:
            moved = pltpu.roll(jnp.where(lane < SHIFTS * h, after, here), LANES - SHIFTS * h, 1)
        turns.append(jnp.concatenate([moved[0:256], moved[8:264]], axis=1).reshape(32, 8, 256))
    shifted[ch] = jnp.stack(turns, axis=1).reshape(1024, 256).astype(BF16)


def correlate(ch, toep, shifted, acc, scale):
    acc[...] = jnp.zeros_like(acc)
    for i in range(16):
        live = 256 - 16 * i
        table = jnp.concatenate([toep[ch, 2 * i], toep[ch, 2 * i + 1]], axis=1)
        part = lax.dot_general(
            shifted[ch, 64 * i : 1024, :],
            table,
            (((1,), (1,)), ((), ())),
            preferred_element_type=F32,
        ).reshape(live // 8, TURNS, 8, 256)
        for h in range(TURNS):
            own = part[:, h].reshape(live, 256)
            acc[h, 0, 0:live] += own[:, :LANES]
            acc[h, 1, 0:live] += own[:, LANES:]
    group = lax.broadcasted_iota(jnp.int32, (256, LANES), 1) // SHIFTS
    total = None
    for turn in range(TURNS):
        mixed = None
        for low in range(TURNS):
            h = (low + turn) % TURNS
            term = acc[h, 0, low : low + 256, :] + acc[h, 1, low + 4 : low + 260, :]
            mixed = term if mixed is None else jnp.where(group == low, term, mixed)
        if turn:
            mixed = pltpu.roll(mixed, SHIFTS * turn, 1)
        total = mixed if total is None else total + mixed
    return total * scale


def channel_row(ref, channel):
    lane = lax.broadcasted_iota(jnp.int32, ref.shape, 1)
    column = jnp.sum(jnp.where(lane == channel, ref[...], 0.0), axis=1, keepdims=True)
    spread = jnp.broadcast_to(column, (16, LANES))
    sub = lax.broadcasted_iota(jnp.int32, (16, LANES), 0)
    lane = lax.broadcasted_iota(jnp.int32, (16, LANES), 1)
    return jnp.sum(jnp.where(lane % 16 == sub, spread, 0.0), axis=0, keepdims=True)


def exchange(
    x_hbm, g_hbm, res_hbm, dec_hbm, recv_c, recv_m,
    x_ref, g_ref, res_ref, dec_ref, stage, send_x, send_g, recv_x, recv_g, grad, toep, tails,
    shifted, acc, send_c, fine, coarse, send_m,
    lsem, ssem_in, rsem_in, ssem_c, rsem_c, ssem_m, rsem_m,
):
    me = lax.axis_index("wide")
    at = place(me)
    peers = [shifted_peer(at, *offset) for offset in OFFSETS]
    scale = 1.0 / math.sqrt(PEERS * x_ref.shape[1])

    barrier = pltpu.get_barrier_semaphore()
    for peer in peers:
        pl.semaphore_signal(barrier, inc=1, device_id={"wide": peer}, device_id_type=MESH)

    fetches = [
        pltpu.make_async_copy(src, dst, lsem.at[n])
        for n, (src, dst) in enumerate(
            ((x_hbm, x_ref), (g_hbm, g_ref), (dec_hbm, dec_ref), (res_hbm, res_ref))
        )
    ]
    for fetch in fetches:
        fetch.start()
    sends, recvs = (send_x, send_g), (recv_x, recv_g)
    for which, ref in enumerate((x_ref, g_ref)):
        fetches[which].wait()
        to_rows(ref, stage, sends[which])
    pl.semaphore_wait(barrier, PEERS - 1)

    def signals_to(which, to, source):
        return pltpu.make_async_remote_copy(
            src_ref=sends[which].at[aligned(to, 16), :],
            dst_ref=recvs[which].at[aligned(source, 16), :],
            send_sem=ssem_in.at[which, to],
            recv_sem=rsem_in.at[which, source],
            device_id={"wide": to},
            device_id_type=MESH,
        )

    for which in range(2):
        for peer in peers:
            signals_to(which, peer, me).start()
    for which in range(2):
        recvs[which][aligned(me, 16), :] = sends[which][aligned(me, 16), :]

    fetches[2].wait()
    fetches[3].wait()
    lane_big = lax.broadcasted_iota(jnp.int32, (256, LANES), 1)
    block_at = (lax.broadcasted_iota(jnp.int32, (256, LANES), 0) * LANES).astype(F32)
    lane_small = lax.broadcasted_iota(jnp.int32, (LANES, LANES), 1)
    offset_at = lax.broadcasted_iota(jnp.int32, (LANES, LANES), 0).astype(F32)
    factors = []
    for ch in range(2):
        rate = channel_row(dec_ref, PEERS * ch + me)
        factors.append(-scale * rate * channel_row(res_ref, PEERS * ch + me))
        own = jnp.logical_and(lane_small >= 64 * ch, lane_small < 64 * ch + 48)
        power = jnp.where(own, jnp.exp(-rate * offset_at), 0.0)
        weighted = jnp.logical_and(lane_small % 64 >= 16, lane_small % 64 < 32)
        power = jnp.where(weighted, offset_at * power, power)
        upper = power.astype(BF16)
        fine[ch, 0] = upper
        fine[ch, 1] = upper
        fine[ch, 2] = (power - upper.astype(F32)).astype(BF16)
        power = jnp.exp(-rate * block_at)
        power = jnp.where(lane_big % 64 < 32, power, block_at * power)
        coarse[:, 64 * ch : 64 * ch + 64] = power[:, 64 * ch : 64 * ch + 64]

    def arrivals(step, first):
        sources = []
        for n in range(4):
            dy, dz = 2 * (step % 2) + n // 2, step // 2
            dy = dy + (dy // 2) * (1 - 2 * (dy % 2))
            dz = dz + (dz // 2) * (1 - 2 * (dz % 2))
            sources.append(shifted_peer(at, dz, dy, n % 2))
        for n, source in enumerate(sources):
            if n or not first:
                signals_to(0, source, source).wait_recv()
        for source in sources:
            build_toeplitz(source, recv_x, toep, tails)

    arrivals(0, True)

    @pl.loop(1, PEERS // 4)
    def _(step):
        arrivals(step, False)

    for ch in range(2):
        toep[ch, 1:, 0:SHIFTS, :] = toep[ch, 1:, 0:SHIFTS, :] + tails[ch, : PEERS - 1]

    @pl.loop(1, PEERS)
    def _(k):
        peer = (me + k) % PEERS
        signals_to(1, peer, peer).wait_recv()

    for ch in range(2):
        rows = recv_g[...].reshape(PEERS, 16, LANES).astype(F32)[:, 8 * ch : 8 * ch + 8]
        grad[ch, 0:256] = rows.reshape(256, LANES)
        grad[ch, 256:] = jnp.zeros((16, LANES), F32)
        build_shifted(ch, grad, shifted)

    def lags_to(ch, to, source):
        return pltpu.make_async_remote_copy(
            src_ref=send_c.at[ch, aligned(to, 8), :],
            dst_ref=recv_c.at[pl.ds(pl.multiple_of(16 * source + 8 * ch, 8), 8), :],
            send_sem=ssem_c.at[ch, to],
            recv_sem=rsem_c.at[ch, source],
            device_id={"wide": to},
            device_id_type=MESH,
        )

    for ch in range(2):
        send_c[ch] = correlate(ch, toep, shifted, acc, scale)
        for peer in peers:
            lags_to(ch, peer, me).start()
        recv_c[pl.ds(pl.multiple_of(16 * me + 8 * ch, 8), 8), :] = send_c[ch, aligned(me, 8), :]

    parts = []
    for ch in range(2):
        lags = send_c[ch]
        upper = lags.astype(BF16)
        parts += [upper, (lags - upper.astype(F32)).astype(BF16), upper]
    mixed = jnp.dot(
        jnp.concatenate(parts, axis=1),
        fine[...].reshape(6 * LANES, LANES),
        preferred_element_type=F32,
    )
    sums = jnp.sum(mixed * coarse[...], axis=0, keepdims=True)
    both = sums + pltpu.roll(sums, LANES - 16, 1)
    lane = lax.broadcasted_iota(jnp.int32, (1, LANES), 1)
    factor = jnp.where(lane < 64, factors[0], factors[1])
    line = jnp.where(lane % 64 < 16, scale * sums, factor * both)
    send_m[...] = line
    recv_m[me] = line

    def modes_to(to, source):
        return pltpu.make_async_remote_copy(
            src_ref=send_m,
            dst_ref=recv_m.at[source],
            send_sem=ssem_m.at[to],
            recv_sem=rsem_m.at[source],
            device_id={"wide": to},
            device_id_type=MESH,
        )

    for peer in peers:
        modes_to(peer, me).start()

    @pl.loop(1, PEERS)
    def _(k):
        peer = (me + k) % PEERS
        signals_to(0, peer, me).wait_send()
        signals_to(1, peer, me).wait_send()
        lags_to(0, peer, me).wait_send()
        lags_to(1, peer, me).wait_send()
        modes_to(peer, me).wait_send()
        lags_to(0, peer, peer).wait_recv()
        lags_to(1, peer, peer).wait_recv()
        modes_to(peer, peer).wait_recv()


def regroup(c_ref, m_ref, out_ref, rg_ref, ld_ref):
    for ch in range(2):
        for k in range(8):
            out_ref[PEERS * ch : PEERS * (ch + 1), k * LANES : (k + 1) * LANES] = c_ref[
                pl.ds(8 * ch + k, PEERS, stride=16), :
            ]
    lines = jnp.transpose(m_ref[:, 0, :])
    rg_ref[...] = jnp.concatenate([lines[0:16], lines[64:80]], axis=1)
    ld_ref[...] = jnp.concatenate([lines[16:32], lines[80:96]], axis=1)


def local(inputs, out_grad, residues, decay):
    chans, block = inputs.shape
    modes = residues.shape[1]
    vmem = pl.BlockSpec(memory_space=pltpu.VMEM)
    hbm = pl.BlockSpec(memory_space=pltpu.HBM)
    dma = pltpu.SemaphoreType.DMA
    lags, lines = pl.pallas_call(
        exchange,
        out_shape=(
            jax.ShapeDtypeStruct((512, LANES), F32),
            jax.ShapeDtypeStruct((PEERS, 1, LANES), F32),
        ),
        in_specs=[hbm] * 4,
        out_specs=(vmem, vmem),
        scratch_shapes=[
            pltpu.VMEM((chans, block), BF16),
            pltpu.VMEM((chans, block), BF16),
            pltpu.VMEM((modes, chans), F32),
            pltpu.VMEM((modes, chans), F32),
            pltpu.VMEM((512, LANES), F32),
            pltpu.VMEM((512, LANES), BF16),
            pltpu.VMEM((512, LANES), BF16),
            pltpu.VMEM((512, LANES), BF16),
            pltpu.VMEM((512, LANES), BF16),
            pltpu.VMEM((2, 272, LANES), F32),
            pltpu.VMEM((2, PEERS, 256, LANES), BF16),
            pltpu.VMEM((2, PEERS, SHIFTS, LANES), BF16),
            pltpu.VMEM((2, 1024, 256), BF16),
            pltpu.VMEM((TURNS, 2, 264, LANES), F32),
            pltpu.VMEM((2, 256, LANES), F32),
            pltpu.VMEM((2, 3, LANES, LANES), BF16),
            pltpu.VMEM((256, LANES), F32),
            pltpu.VMEM((1, LANES), F32),
            dma((4,)),
            dma((2, PEERS)),
            dma((2, PEERS)),
            dma((2, PEERS)),
            dma((2, PEERS)),
            dma((PEERS,)),
            dma((PEERS,)),
        ],
        compiler_params=pltpu.CompilerParams(
            collective_id=0, has_side_effects=True, vmem_limit_bytes=32 * 2**20
        ),
    )(*(pltpu.with_memory_space_constraint(a, pltpu.HBM) for a in (inputs, out_grad, residues.T, decay.T)))
    filter_grad, residue_grad, log_decay_grad = pl.pallas_call(
        regroup,
        out_shape=(
            jax.ShapeDtypeStruct((chans, block), F32),
            jax.ShapeDtypeStruct((modes, chans), F32),
            jax.ShapeDtypeStruct((modes, chans), F32),
        ),
        in_specs=[vmem] * 2,
        out_specs=(vmem,) * 3,
        compiler_params=pltpu.CompilerParams(vmem_limit_bytes=4 * 2**20),
    )(lags, lines)
    return filter_grad, residue_grad.T, log_decay_grad.T


def solution(mesh):
    placed = (P("narrow", "wide"), P("narrow", "wide"), P("narrow", None), P("narrow", None))
    return jax.shard_map(
        local,
        mesh=mesh,
        in_specs=placed,
        out_specs=(P("narrow", "wide"), P("narrow", None), P("narrow", None)),
        check_vma=False,
    )
```

```python
import math

import jax
import jax.numpy as jnp
from jax import lax
from jax.experimental import pallas as pl
from jax.experimental.pallas import tpu as pltpu
from jax.sharding import PartitionSpec as P

F32 = jnp.float32
BF16 = jnp.bfloat16
MESH = pl.DeviceIdType.MESH

LANES = 128
SHIFTS = 32
TURNS = LANES // SHIFTS
PEERS = 32
RING = (0, 1, 2, 1)
NEAR = (0, 1, 3, 2)
OFFSETS = sorted(
    ((dz, dy, dc) for dz in range(4) for dy in range(4) for dc in range(2) if dz or dy or dc),
    key=lambda o: (-RING[o[0]] - RING[o[1]], -o[2], o),
)


def place(me):
    return me // 8, (me // 2) % 4, me % 2


def shifted_peer(at, dz, dy, dc):
    z, y, core = at
    return ((z + dz) % 4) * 8 + ((y + dy) % 4) * 2 + (core + dc) % 2


def group_of(dz, dy, dc):
    return 2 * NEAR.index(dz) + NEAR.index(dy) // 2


def aligned(index, size):
    return pl.ds(pl.multiple_of(index * size, size), size)


def to_rows(block_ref, which, stage):
    for ch in range(2):
        for k in range(8):
            stage[pl.ds(16 * which + 8 * ch + k, PEERS, stride=32), :] = block_ref[
                PEERS * ch : PEERS * (ch + 1), k * LANES : (k + 1) * LANES
            ].astype(F32)


def wait_rows(ref, rows, sem):
    part = ref.at[0:rows]
    pltpu.make_async_copy(part, part, sem).wait()


def build_toeplitz(j, recv, toep, tails):
    row = lax.broadcasted_iota(jnp.int32, (SHIFTS, LANES), 0)
    lane = lax.broadcasted_iota(jnp.int32, (SHIFTS, LANES), 1)
    keep = lane >= row
    block = recv[pl.ds(pl.multiple_of(32 * j, 32), 16), :].astype(F32)
    for ch in range(2):
        before = jnp.zeros((SHIFTS, LANES), F32)
        for q in range(8):
            spread = jnp.broadcast_to(block[8 * ch + q : 8 * ch + q + 1], (SHIFTS, LANES))
            now = pltpu.roll(spread, 0, 1, stride=1, stride_axis=0)
            toep[ch, j, q * SHIFTS : (q + 1) * SHIFTS, :] = jnp.where(keep, now, before).astype(BF16)
            before = now
        tails[ch, j] = jnp.where(keep, 0.0, before).astype(BF16)


def build_shifted(ch, grad, shifted):
    lane = lax.broadcasted_iota(jnp.int32, (264, LANES), 1)
    here = grad[ch, 0:264, :]
    after = grad[ch, 1:265, :]
    turns = []
    for h in range(TURNS):
        moved = here
        if h:
            moved = pltpu.roll(jnp.where(lane < SHIFTS * h, after, here), LANES - SHIFTS * h, 1)
        turns.append(jnp.concatenate([moved[0:256], moved[8:264]], axis=1).reshape(32, 8, 256))
    shifted[ch] = jnp.stack(turns, axis=1).reshape(1024, 256).astype(BF16)


def correlate(ch, toep, shifted, acc, scale):
    acc[...] = jnp.zeros_like(acc)
    for i in range(16):
        live = 256 - 16 * i
        table = jnp.concatenate([toep[ch, 2 * i], toep[ch, 2 * i + 1]], axis=1)
        part = lax.dot_general(
            shifted[ch, 64 * i : 1024, :],
            table,
            (((1,), (1,)), ((), ())),
            preferred_element_type=F32,
        ).reshape(live // 8, TURNS, 8, 256)
        for h in range(TURNS):
            own = part[:, h].reshape(live, 256)
            acc[h, 0, 0:live] += own[:, :LANES]
            acc[h, 1, 0:live] += own[:, LANES:]
    group = lax.broadcasted_iota(jnp.int32, (256, LANES), 1) // SHIFTS
    total = None
    for turn in range(TURNS):
        mixed = None
        for low in range(TURNS):
            h = (low + turn) % TURNS
            term = acc[h, 0, low : low + 256, :] + acc[h, 1, low + 4 : low + 260, :]
            mixed = term if mixed is None else jnp.where(group == low, term, mixed)
        if turn:
            mixed = pltpu.roll(mixed, SHIFTS * turn, 1)
        total = mixed if total is None else total + mixed
    return total * scale


def channel_row(ref, channel):
    lane = lax.broadcasted_iota(jnp.int32, ref.shape, 1)
    column = jnp.sum(jnp.where(lane == channel, ref[...], 0.0), axis=1, keepdims=True)
    spread = jnp.broadcast_to(column, (16, LANES))
    sub = lax.broadcasted_iota(jnp.int32, (16, LANES), 0)
    lane = lax.broadcasted_iota(jnp.int32, (16, LANES), 1)
    return jnp.sum(jnp.where(lane % 16 == sub, spread, 0.0), axis=0, keepdims=True)


def exchange(
    x_hbm, g_hbm, res_hbm, dec_hbm, recv_c, recv_m,
    x_ref, g_ref, res_ref, dec_ref, stage, send, recv, grad, toep, tails, shifted,
    acc, send_c, fine, coarse, send_m,
    fetched, sent_in, come_in, sent_c, come_c, sent_m, come_m,
):
    me = lax.axis_index("wide")
    at = place(me)
    peers = [shifted_peer(at, *offset) for offset in OFFSETS]
    scale = 1.0 / math.sqrt(PEERS * x_ref.shape[1])

    barrier = pltpu.get_barrier_semaphore()
    for peer in peers:
        pl.semaphore_signal(barrier, inc=1, device_id={"wide": peer}, device_id_type=MESH)

    fetches = [
        pltpu.make_async_copy(src, dst, fetched.at[n])
        for n, (src, dst) in enumerate(
            ((x_hbm, x_ref), (g_hbm, g_ref), (dec_hbm, dec_ref), (res_hbm, res_ref))
        )
    ]
    for fetch in fetches:
        fetch.start()
    for which, ref in enumerate((x_ref, g_ref)):
        fetches[which].wait()
        to_rows(ref, which, stage)
    send[...] = stage[...].astype(BF16)
    pl.semaphore_wait(barrier, PEERS - 1)

    for peer, offset in zip(peers, OFFSETS):
        back = tuple(-d % n for d, n in zip(offset, (4, 4, 2)))
        pltpu.make_async_remote_copy(
            src_ref=send.at[aligned(peer, 32), :],
            dst_ref=recv.at[aligned(me, 32), :],
            send_sem=sent_in,
            recv_sem=come_in.at[group_of(*back)],
            device_id={"wide": peer},
            device_id_type=MESH,
        ).start()
    recv[aligned(me, 32), :] = send[aligned(me, 32), :]

    fetches[2].wait()
    fetches[3].wait()
    lane_big = lax.broadcasted_iota(jnp.int32, (256, LANES), 1)
    block_at = (lax.broadcasted_iota(jnp.int32, (256, LANES), 0) * LANES).astype(F32)
    lane_small = lax.broadcasted_iota(jnp.int32, (LANES, LANES), 1)
    offset_at = lax.broadcasted_iota(jnp.int32, (LANES, LANES), 0).astype(F32)
    factors = []
    for ch in range(2):
        rate = channel_row(dec_ref, PEERS * ch + me)
        factors.append(-scale * rate * channel_row(res_ref, PEERS * ch + me))
        own = jnp.logical_and(lane_small >= 64 * ch, lane_small < 64 * ch + 48)
        power = jnp.where(own, jnp.exp(-rate * offset_at), 0.0)
        weighted = jnp.logical_and(lane_small % 64 >= 16, lane_small % 64 < 32)
        power = jnp.where(weighted, offset_at * power, power)
        upper = power.astype(BF16)
        fine[ch, 0] = upper
        fine[ch, 1] = upper
        fine[ch, 2] = (power - upper.astype(F32)).astype(BF16)
        power = jnp.exp(-rate * block_at)
        power = jnp.where(lane_big % 64 < 32, power, block_at * power)
        coarse[:, 64 * ch : 64 * ch + 64] = power[:, 64 * ch : 64 * ch + 64]

    def arrivals(group, senders):
        wait_rows(recv, 32 * senders, come_in.at[group])
        for n in range(4):
            dy, dz = 2 * (group % 2) + n // 2, group // 2
            dy = dy + (dy // 2) * (1 - 2 * (dy % 2))
            dz = dz + (dz // 2) * (1 - 2 * (dz % 2))
            build_toeplitz(shifted_peer(at, dz, dy, n % 2), recv, toep, tails)

    arrivals(0, 3)

    @pl.loop(1, 8)
    def _(group):
        arrivals(group, 4)

    for ch in range(2):
        toep[ch, 1:, 0:SHIFTS, :] = toep[ch, 1:, 0:SHIFTS, :] + tails[ch, : PEERS - 1]

    for ch in range(2):
        rows = recv[...].reshape(PEERS, 32, LANES)[:, 16:32].astype(F32)[:, 8 * ch : 8 * ch + 8]
        grad[ch, 0:256] = rows.reshape(256, LANES)
        grad[ch, 256:] = jnp.zeros((16, LANES), F32)
        build_shifted(ch, grad, shifted)

    for ch in range(2):
        lags = correlate(ch, toep, shifted, acc, scale)
        send_c[:, 8 * ch : 8 * ch + 8, :] = lags.reshape(PEERS, 8, LANES)
    for peer in peers:
        pltpu.make_async_remote_copy(
            src_ref=send_c.at[peer],
            dst_ref=recv_c.at[me],
            send_sem=sent_c,
            recv_sem=come_c,
            device_id={"wide": peer},
            device_id_type=MESH,
        ).start()
    recv_c[me] = send_c[me]

    parts = []
    for ch in range(2):
        lags = send_c[:, 8 * ch : 8 * ch + 8, :].reshape(256, LANES)
        upper = lags.astype(BF16)
        parts += [upper, (lags - upper.astype(F32)).astype(BF16), upper]
    mixed = jnp.dot(
        jnp.concatenate(parts, axis=1),
        fine[...].reshape(6 * LANES, LANES),
        preferred_element_type=F32,
    )
    sums = jnp.sum(mixed * coarse[...], axis=0, keepdims=True)
    both = sums + pltpu.roll(sums, LANES - 16, 1)
    lane = lax.broadcasted_iota(jnp.int32, (1, LANES), 1)
    factor = jnp.where(lane < 64, factors[0], factors[1])
    line = jnp.where(lane % 64 < 16, scale * sums, factor * both)
    send_m[...] = line
    recv_m[me] = line

    for peer in peers:
        pltpu.make_async_remote_copy(
            src_ref=send_m,
            dst_ref=recv_m.at[me],
            send_sem=sent_m,
            recv_sem=come_m,
            device_id={"wide": peer},
            device_id_type=MESH,
        ).start()

    wait_rows(send, 32 * (PEERS - 1), sent_in)
    wait_rows(send_c, PEERS - 1, sent_c)
    wait_rows(recv_m, PEERS - 1, sent_m)
    wait_rows(recv_c, PEERS - 1, come_c)
    wait_rows(recv_m, PEERS - 1, come_m)


def regroup(c_ref, m_ref, out_ref, rg_ref, ld_ref):
    for ch in range(2):
        for k in range(8):
            out_ref[PEERS * ch : PEERS * (ch + 1), k * LANES : (k + 1) * LANES] = c_ref[
                :, 8 * ch + k, :
            ]
    lines = jnp.transpose(m_ref[:, 0, :])
    rg_ref[...] = jnp.concatenate([lines[0:16], lines[64:80]], axis=1)
    ld_ref[...] = jnp.concatenate([lines[16:32], lines[80:96]], axis=1)


def local(inputs, out_grad, residues, decay):
    chans, block = inputs.shape
    modes = residues.shape[1]
    vmem = pl.BlockSpec(memory_space=pltpu.VMEM)
    hbm = pl.BlockSpec(memory_space=pltpu.HBM)
    dma = pltpu.SemaphoreType.DMA
    lags, lines = pl.pallas_call(
        exchange,
        out_shape=(
            jax.ShapeDtypeStruct((PEERS, 16, LANES), F32),
            jax.ShapeDtypeStruct((PEERS, 1, LANES), F32),
        ),
        in_specs=[hbm] * 4,
        out_specs=(vmem, vmem),
        scratch_shapes=[
            pltpu.VMEM((chans, block), BF16),
            pltpu.VMEM((chans, block), BF16),
            pltpu.VMEM((modes, chans), F32),
            pltpu.VMEM((modes, chans), F32),
            pltpu.VMEM((1024, LANES), F32),
            pltpu.VMEM((1024, LANES), BF16),
            pltpu.VMEM((1024, LANES), BF16),
            pltpu.VMEM((2, 272, LANES), F32),
            pltpu.VMEM((2, PEERS, 256, LANES), BF16),
            pltpu.VMEM((2, PEERS, SHIFTS, LANES), BF16),
            pltpu.VMEM((2, 1024, 256), BF16),
            pltpu.VMEM((TURNS, 2, 264, LANES), F32),
            pltpu.VMEM((PEERS, 16, LANES), F32),
            pltpu.VMEM((2, 3, LANES, LANES), BF16),
            pltpu.VMEM((256, LANES), F32),
            pltpu.VMEM((1, LANES), F32),
            dma((4,)),
            dma,
            dma((8,)),
            dma,
            dma,
            dma,
            dma,
        ],
        compiler_params=pltpu.CompilerParams(
            collective_id=0, has_side_effects=True, vmem_limit_bytes=32 * 2**20
        ),
    )(*(pltpu.with_memory_space_constraint(a, pltpu.HBM) for a in (inputs, out_grad, residues.T, decay.T)))
    filter_grad, residue_grad, log_decay_grad = pl.pallas_call(
        regroup,
        out_shape=(
            jax.ShapeDtypeStruct((chans, block), F32),
            jax.ShapeDtypeStruct((modes, chans), F32),
            jax.ShapeDtypeStruct((modes, chans), F32),
        ),
        in_specs=[vmem] * 2,
        out_specs=(vmem,) * 3,
        compiler_params=pltpu.CompilerParams(vmem_limit_bytes=4 * 2**20),
    )(lags, lines)
    return filter_grad, residue_grad.T, log_decay_grad.T


def solution(mesh):
    placed = (P("narrow", "wide"), P("narrow", "wide"), P("narrow", None), P("narrow", None))
    return jax.shard_map(
        local,
        mesh=mesh,
        in_specs=placed,
        out_specs=(P("narrow", "wide"), P("narrow", None), P("narrow", None)),
        check_vma=False,
    )
```

```python
import math

import jax
import jax.numpy as jnp
from jax import lax
from jax.experimental import pallas as pl
from jax.experimental.pallas import tpu as pltpu
from jax.sharding import PartitionSpec as P

F32 = jnp.float32
BF16 = jnp.bfloat16
MESH = pl.DeviceIdType.MESH

LANES = 128
SHIFTS = 32
TURNS = LANES // SHIFTS
PEERS = 32
RING = (0, 1, 2, 1)
OFFSETS = sorted(
    ((dz, dy, dc) for dz in range(4) for dy in range(4) for dc in range(2) if dz or dy or dc),
    key=lambda o: (-RING[o[0]] - RING[o[1]], -o[2], o),
)


def place(me):
    return me // 8, (me // 2) % 4, me % 2


def shifted_peer(at, dz, dy, dc):
    z, y, core = at
    return ((z + dz) % 4) * 8 + ((y + dy) % 4) * 2 + (core + dc) % 2


def aligned(index, size):
    return pl.ds(pl.multiple_of(index * size, size), size)


def to_rows(block_ref, which, stage):
    for ch in range(2):
        for k in range(8):
            stage[pl.ds(16 * which + 8 * ch + k, PEERS, stride=32), :] = block_ref[
                PEERS * ch : PEERS * (ch + 1), k * LANES : (k + 1) * LANES
            ].astype(F32)


def wait_rows(ref, rows, sem):
    part = ref.at[0:rows]
    pltpu.make_async_copy(part, part, sem).wait()


def toeplitz(ch, i, signal, before):
    row = lax.broadcasted_iota(jnp.int32, (SHIFTS, LANES), 0)
    lane = lax.broadcasted_iota(jnp.int32, (SHIFTS, LANES), 1)
    halves = []
    for p in range(2):
        rows = []
        for q in range(8):
            spread = jnp.broadcast_to(signal[ch, pl.ds(16 * i + 8 * p + q, 1), :], (SHIFTS, LANES))
            now = pltpu.roll(spread, 0, 1, stride=1, stride_axis=0)
            rows.append(jnp.where(lane >= row, now, before).astype(BF16))
            before = now
        halves.append(jnp.concatenate(rows, axis=0))
    return jnp.concatenate(halves, axis=1), before


def build_shifted(ch, grad, shifted):
    lane = lax.broadcasted_iota(jnp.int32, (264, LANES), 1)
    here = grad[ch, 0:264, :]
    after = grad[ch, 1:265, :]
    turns = []
    for h in range(TURNS):
        moved = here
        if h:
            moved = pltpu.roll(jnp.where(lane < SHIFTS * h, after, here), LANES - SHIFTS * h, 1)
        turns.append(jnp.concatenate([moved[0:256], moved[8:264]], axis=1).reshape(32, 8, 256))
    shifted[ch] = jnp.stack(turns, axis=1).reshape(1024, 256).astype(BF16)


def correlate(ch, signal, shifted, acc, scale):
    acc[:, :, 256:, :] = jnp.zeros((TURNS, 2, 8, LANES), F32)
    before = jnp.zeros((SHIFTS, LANES), F32)
    for i in range(16):
        live = 256 - 16 * i
        table, before = toeplitz(ch, i, signal, before)
        part = lax.dot_general(
            shifted[ch, 64 * i : 1024, :],
            table,
            (((1,), (1,)), ((), ())),
            preferred_element_type=F32,
        ).reshape(live // 8, TURNS, 8, 256)
        for h in range(TURNS):
            own = part[:, h].reshape(live, 256)
            for half in range(2):
                term = own[:, half * LANES : (half + 1) * LANES]
                acc[h, half, 0:live] = acc[h, half, 0:live] + term if i else term
    group = lax.broadcasted_iota(jnp.int32, (256, LANES), 1) // SHIFTS
    total = None
    for turn in range(TURNS):
        mixed = None
        for low in range(TURNS):
            h = (low + turn) % TURNS
            term = acc[h, 0, low : low + 256, :] + acc[h, 1, low + 4 : low + 260, :]
            mixed = term if mixed is None else jnp.where(group == low, term, mixed)
        if turn:
            mixed = pltpu.roll(mixed, SHIFTS * turn, 1)
        total = mixed if total is None else total + mixed
    return total * scale


def channel_row(ref, channel):
    lane = lax.broadcasted_iota(jnp.int32, ref.shape, 1)
    column = jnp.sum(jnp.where(lane == channel, ref[...], 0.0), axis=1, keepdims=True)
    spread = jnp.broadcast_to(column, (16, LANES))
    sub = lax.broadcasted_iota(jnp.int32, (16, LANES), 0)
    lane = lax.broadcasted_iota(jnp.int32, (16, LANES), 1)
    return jnp.sum(jnp.where(lane % 16 == sub, spread, 0.0), axis=0, keepdims=True)


def exchange(
    x_hbm, g_hbm, res_hbm, dec_hbm, recv_c, recv_m,
    x_ref, g_ref, res_ref, dec_ref, stage, send, recv, signal, grad, shifted,
    acc, send_c, fine, coarse, send_m,
    fetched, sent_in, come_in, sent_c, come_c, sent_m, come_m,
):
    me = lax.axis_index("wide")
    at = place(me)
    peers = [shifted_peer(at, *offset) for offset in OFFSETS]
    scale = 1.0 / math.sqrt(PEERS * x_ref.shape[1])

    barrier = pltpu.get_barrier_semaphore()
    for peer in peers:
        pl.semaphore_signal(barrier, inc=1, device_id={"wide": peer}, device_id_type=MESH)

    fetches = [
        pltpu.make_async_copy(src, dst, fetched.at[n])
        for n, (src, dst) in enumerate(
            ((x_hbm, x_ref), (g_hbm, g_ref), (dec_hbm, dec_ref), (res_hbm, res_ref))
        )
    ]
    for fetch in fetches:
        fetch.start()
    for which, ref in enumerate((x_ref, g_ref)):
        fetches[which].wait()
        to_rows(ref, which, stage)
    send[...] = stage[...].astype(BF16)
    pl.semaphore_wait(barrier, PEERS - 1)

    for peer in peers:
        pltpu.make_async_remote_copy(
            src_ref=send.at[aligned(peer, 32), :],
            dst_ref=recv.at[aligned(me, 32), :],
            send_sem=sent_in,
            recv_sem=come_in,
            device_id={"wide": peer},
            device_id_type=MESH,
        ).start()
    recv[aligned(me, 32), :] = send[aligned(me, 32), :]

    fetches[2].wait()
    fetches[3].wait()
    lane_big = lax.broadcasted_iota(jnp.int32, (256, LANES), 1)
    block_at = (lax.broadcasted_iota(jnp.int32, (256, LANES), 0) * LANES).astype(F32)
    lane_small = lax.broadcasted_iota(jnp.int32, (LANES, LANES), 1)
    offset_at = lax.broadcasted_iota(jnp.int32, (LANES, LANES), 0).astype(F32)
    factors = []
    for ch in range(2):
        rate = channel_row(dec_ref, PEERS * ch + me)
        factors.append(-scale * rate * channel_row(res_ref, PEERS * ch + me))
        own = jnp.logical_and(lane_small >= 64 * ch, lane_small < 64 * ch + 48)
        power = jnp.where(own, jnp.exp(-rate * offset_at), 0.0)
        weighted = jnp.logical_and(lane_small % 64 >= 16, lane_small % 64 < 32)
        power = jnp.where(weighted, offset_at * power, power)
        upper = power.astype(BF16)
        fine[ch, 0] = upper
        fine[ch, 1] = upper
        fine[ch, 2] = (power - upper.astype(F32)).astype(BF16)
        power = jnp.exp(-rate * block_at)
        power = jnp.where(lane_big % 64 < 32, power, block_at * power)
        coarse[:, 64 * ch : 64 * ch + 64] = power[:, 64 * ch : 64 * ch + 64]

    wait_rows(recv, 32 * (PEERS - 1), come_in)
    for ch in range(2):
        rows = recv[...].astype(F32).reshape(PEERS, 32, LANES)
        signal[ch] = rows[:, 8 * ch : 8 * ch + 8].reshape(256, LANES)
        grad[ch, 0:256] = rows[:, 8 * ch + 16 : 8 * ch + 24].reshape(256, LANES)
        grad[ch, 256:] = jnp.zeros((16, LANES), F32)
        build_shifted(ch, grad, shifted)

    for ch in range(2):
        lags = correlate(ch, signal, shifted, acc, scale)
        send_c[:, 8 * ch : 8 * ch + 8, :] = lags.reshape(PEERS, 8, LANES)
    for peer in peers:
        pltpu.make_async_remote_copy(
            src_ref=send_c.at[peer],
            dst_ref=recv_c.at[me],
            send_sem=sent_c,
            recv_sem=come_c,
            device_id={"wide": peer},
            device_id_type=MESH,
        ).start()
    recv_c[me] = send_c[me]

    parts = []
    for ch in range(2):
        lags = send_c[:, 8 * ch : 8 * ch + 8, :].reshape(256, LANES)
        upper = lags.astype(BF16)
        parts += [upper, (lags - upper.astype(F32)).astype(BF16), upper]
    mixed = jnp.dot(
        jnp.concatenate(parts, axis=1),
        fine[...].reshape(6 * LANES, LANES),
        preferred_element_type=F32,
    )
    sums = jnp.sum(mixed * coarse[...], axis=0, keepdims=True)
    both = sums + pltpu.roll(sums, LANES - 16, 1)
    lane = lax.broadcasted_iota(jnp.int32, (1, LANES), 1)
    factor = jnp.where(lane < 64, factors[0], factors[1])
    line = jnp.where(lane % 64 < 16, scale * sums, factor * both)
    send_m[...] = line
    recv_m[me] = line

    for peer in peers:
        pltpu.make_async_remote_copy(
            src_ref=send_m,
            dst_ref=recv_m.at[me],
            send_sem=sent_m,
            recv_sem=come_m,
            device_id={"wide": peer},
            device_id_type=MESH,
        ).start()

    wait_rows(send, 32 * (PEERS - 1), sent_in)
    wait_rows(send_c, PEERS - 1, sent_c)
    wait_rows(recv_m, PEERS - 1, sent_m)
    wait_rows(recv_c, PEERS - 1, come_c)
    wait_rows(recv_m, PEERS - 1, come_m)


def regroup(c_ref, m_ref, out_ref, rg_ref, ld_ref):
    for ch in range(2):
        for k in range(8):
            out_ref[PEERS * ch : PEERS * (ch + 1), k * LANES : (k + 1) * LANES] = c_ref[
                :, 8 * ch + k, :
            ]
    lines = jnp.transpose(m_ref[:, 0, :])
    rg_ref[...] = jnp.concatenate([lines[0:16], lines[64:80]], axis=1)
    ld_ref[...] = jnp.concatenate([lines[16:32], lines[80:96]], axis=1)


def local(inputs, out_grad, residues, decay):
    chans, block = inputs.shape
    modes = residues.shape[1]
    vmem = pl.BlockSpec(memory_space=pltpu.VMEM)
    hbm = pl.BlockSpec(memory_space=pltpu.HBM)
    dma = pltpu.SemaphoreType.DMA
    lags, lines = pl.pallas_call(
        exchange,
        out_shape=(
            jax.ShapeDtypeStruct((PEERS, 16, LANES), F32),
            jax.ShapeDtypeStruct((PEERS, 1, LANES), F32),
        ),
        in_specs=[hbm] * 4,
        out_specs=(vmem, vmem),
        scratch_shapes=[
            pltpu.VMEM((chans, block), BF16),
            pltpu.VMEM((chans, block), BF16),
            pltpu.VMEM((modes, chans), F32),
            pltpu.VMEM((modes, chans), F32),
            pltpu.VMEM((1024, LANES), F32),
            pltpu.VMEM((1024, LANES), BF16),
            pltpu.VMEM((1024, LANES), BF16),
            pltpu.VMEM((2, 256, LANES), F32),
            pltpu.VMEM((2, 272, LANES), F32),
            pltpu.VMEM((2, 1024, 256), BF16),
            pltpu.VMEM((TURNS, 2, 264, LANES), F32),
            pltpu.VMEM((PEERS, 16, LANES), F32),
            pltpu.VMEM((2, 3, LANES, LANES), BF16),
            pltpu.VMEM((256, LANES), F32),
            pltpu.VMEM((1, LANES), F32),
            dma((4,)),
            dma,
            dma,
            dma,
            dma,
            dma,
            dma,
        ],
        compiler_params=pltpu.CompilerParams(
            collective_id=0, has_side_effects=True, vmem_limit_bytes=32 * 2**20
        ),
    )(*(pltpu.with_memory_space_constraint(a, pltpu.HBM) for a in (inputs, out_grad, residues.T, decay.T)))
    filter_grad, residue_grad, log_decay_grad = pl.pallas_call(
        regroup,
        out_shape=(
            jax.ShapeDtypeStruct((chans, block), F32),
            jax.ShapeDtypeStruct((modes, chans), F32),
            jax.ShapeDtypeStruct((modes, chans), F32),
        ),
        in_specs=[vmem] * 2,
        out_specs=(vmem,) * 3,
        compiler_params=pltpu.CompilerParams(vmem_limit_bytes=4 * 2**20),
    )(lags, lines)
    return filter_grad, residue_grad.T, log_decay_grad.T


def solution(mesh):
    placed = (P("narrow", "wide"), P("narrow", "wide"), P("narrow", None), P("narrow", None))
    return jax.shard_map(
        local,
        mesh=mesh,
        in_specs=placed,
        out_specs=(P("narrow", "wide"), P("narrow", None), P("narrow", None)),
        check_vma=False,
    )
```

```python
import math

import jax
import jax.numpy as jnp
from jax import lax
from jax.experimental import pallas as pl
from jax.experimental.pallas import tpu as pltpu
from jax.sharding import PartitionSpec as P

F32 = jnp.float32
BF16 = jnp.bfloat16
MESH = pl.DeviceIdType.MESH

LANES = 128
SHIFTS = 32
TURNS = LANES // SHIFTS
PEERS = 32
RING = (0, 1, 2, 1)
OFFSETS = sorted(
    ((dz, dy, dc) for dz in range(4) for dy in range(4) for dc in range(2) if dz or dy or dc),
    key=lambda o: (-RING[o[0]] - RING[o[1]], -o[2], o),
)


def place(me):
    return me // 8, (me // 2) % 4, me % 2


def shifted_peer(at, dz, dy, dc):
    z, y, core = at
    return ((z + dz) % 4) * 8 + ((y + dy) % 4) * 2 + (core + dc) % 2


def aligned(index, size):
    return pl.ds(pl.multiple_of(index * size, size), size)


def to_rows(block_ref, which, stage):
    for ch in range(2):
        for k in range(8):
            stage[pl.ds(16 * which + 8 * ch + k, PEERS, stride=32), :] = block_ref[
                PEERS * ch : PEERS * (ch + 1), k * LANES : (k + 1) * LANES
            ].astype(F32)


def wait_rows(ref, rows, sem):
    part = ref.at[0:rows]
    pltpu.make_async_copy(part, part, sem).wait()


def turned(ch, m, signal):
    if m < 0:
        return jnp.zeros((SHIFTS, LANES), F32)
    spread = jnp.broadcast_to(signal[ch, pl.ds(m, 1), :], (SHIFTS, LANES))
    return pltpu.roll(spread, 0, 1, stride=1, stride_axis=0)


def toeplitz(ch, i, signal, now):
    row = lax.broadcasted_iota(jnp.int32, (SHIFTS, LANES), 0)
    lane = lax.broadcasted_iota(jnp.int32, (SHIFTS, LANES), 1)
    rows = []
    for m in range(16 * i + 15, 16 * i - 1, -1):
        before = turned(ch, m - 1, signal)
        rows.insert(0, jnp.where(lane >= row, now, before).astype(BF16))
        now = before
    halves = [jnp.concatenate(rows[:8], axis=0), jnp.concatenate(rows[8:], axis=0)]
    return jnp.concatenate(halves, axis=1), now


def build_shifted(ch, plane, grad, shifted):
    first = 64 * plane
    lane = lax.broadcasted_iota(jnp.int32, (72, LANES), 1)
    here = grad[ch, first : first + 72, :]
    after = grad[ch, first + 1 : first + 73, :]
    turns = []
    for h in range(TURNS):
        moved = here
        if h:
            moved = pltpu.roll(jnp.where(lane < SHIFTS * h, after, here), LANES - SHIFTS * h, 1)
        turns.append(jnp.concatenate([moved[0:64], moved[8:72]], axis=1).reshape(8, 8, 256))
    shifted[ch, 4 * first : 4 * first + 256] = (
        jnp.stack(turns, axis=1).reshape(256, 256).astype(BF16)
    )


def add_chunk(ch, i, signal, shifted, acc, now):
    live = 256 - 16 * i
    table, now = toeplitz(ch, i, signal, now)
    part = lax.dot_general(
        shifted[ch, 64 * i : 1024, :],
        table,
        (((1,), (1,)), ((), ())),
        preferred_element_type=F32,
    ).reshape(live // 8, TURNS, 8, 256)
    for h in range(TURNS):
        own = part[:, h].reshape(live, 256)
        for half in range(2):
            term = own[:, half * LANES : (half + 1) * LANES]
            if live > 16:
                acc[ch, h, half, 0 : live - 16] = acc[ch, h, half, 0 : live - 16] + term[: live - 16]
            acc[ch, h, half, live - 16 : live] = term[live - 16 :]
    return now


def regroup_lags(ch, acc, scale):
    group = lax.broadcasted_iota(jnp.int32, (256, LANES), 1) // SHIFTS
    total = None
    for turn in range(TURNS):
        mixed = None
        for low in range(TURNS):
            h = (low + turn) % TURNS
            term = acc[ch, h, 0, low : low + 256, :] + acc[ch, h, 1, low + 4 : low + 260, :]
            mixed = term if mixed is None else jnp.where(group == low, term, mixed)
        if turn:
            mixed = pltpu.roll(mixed, SHIFTS * turn, 1)
        total = mixed if total is None else total + mixed
    return total * scale


def channel_row(ref, channel):
    lane = lax.broadcasted_iota(jnp.int32, ref.shape, 1)
    column = jnp.sum(jnp.where(lane == channel, ref[...], 0.0), axis=1, keepdims=True)
    spread = jnp.broadcast_to(column, (16, LANES))
    sub = lax.broadcasted_iota(jnp.int32, (16, LANES), 0)
    lane = lax.broadcasted_iota(jnp.int32, (16, LANES), 1)
    return jnp.sum(jnp.where(lane % 16 == sub, spread, 0.0), axis=0, keepdims=True)


def exchange(
    x_hbm, g_hbm, res_hbm, dec_hbm, recv_c, recv_m,
    x_ref, g_ref, res_ref, dec_ref, stage, send, recv, signal, grad, shifted,
    acc, send_c, fine, coarse, send_m,
    fetched, sent_in, come_in, sent_c, come_c, sent_m, come_m,
):
    me = lax.axis_index("wide")
    at = place(me)
    peers = [shifted_peer(at, *offset) for offset in OFFSETS]
    scale = 1.0 / math.sqrt(PEERS * x_ref.shape[1])

    barrier = pltpu.get_barrier_semaphore()
    for peer in peers:
        pl.semaphore_signal(barrier, inc=1, device_id={"wide": peer}, device_id_type=MESH)

    fetches = [
        pltpu.make_async_copy(src, dst, fetched.at[n])
        for n, (src, dst) in enumerate(
            ((x_hbm, x_ref), (g_hbm, g_ref), (dec_hbm, dec_ref), (res_hbm, res_ref))
        )
    ]
    for fetch in fetches:
        fetch.start()
    for which, ref in enumerate((x_ref, g_ref)):
        fetches[which].wait()
        to_rows(ref, which, stage)
    send[...] = stage[...].astype(BF16)
    pl.semaphore_wait(barrier, PEERS - 1)

    for peer in peers:
        pltpu.make_async_remote_copy(
            src_ref=send.at[aligned(peer, 32), :],
            dst_ref=recv.at[aligned(me, 32), :],
            send_sem=sent_in,
            recv_sem=come_in.at[me // 8],
            device_id={"wide": peer},
            device_id_type=MESH,
        ).start()
    own = pltpu.make_async_copy(
        send.at[aligned(me, 32), :], recv.at[aligned(me, 32), :], come_in.at[me // 8]
    )
    own.start()

    fetches[2].wait()
    fetches[3].wait()
    lane_big = lax.broadcasted_iota(jnp.int32, (256, LANES), 1)
    block_at = (lax.broadcasted_iota(jnp.int32, (256, LANES), 0) * LANES).astype(F32)
    lane_small = lax.broadcasted_iota(jnp.int32, (LANES, LANES), 1)
    offset_at = lax.broadcasted_iota(jnp.int32, (LANES, LANES), 0).astype(F32)
    factors = []
    for ch in range(2):
        rate = channel_row(dec_ref, PEERS * ch + me)
        factors.append(-scale * rate * channel_row(res_ref, PEERS * ch + me))
        own = jnp.logical_and(lane_small >= 64 * ch, lane_small < 64 * ch + 48)
        power = jnp.where(own, jnp.exp(-rate * offset_at), 0.0)
        weighted = jnp.logical_and(lane_small % 64 >= 16, lane_small % 64 < 32)
        power = jnp.where(weighted, offset_at * power, power)
        upper = power.astype(BF16)
        fine[ch, 0] = upper
        fine[ch, 1] = upper
        fine[ch, 2] = (power - upper.astype(F32)).astype(BF16)
        power = jnp.exp(-rate * block_at)
        power = jnp.where(lane_big % 64 < 32, power, block_at * power)
        coarse[:, 64 * ch : 64 * ch + 64] = power[:, 64 * ch : 64 * ch + 64]

    grad[:, 256:] = jnp.zeros((2, 16, LANES), F32)
    acc[:, :, :, 256:] = jnp.zeros((2, TURNS, 2, 8, LANES), F32)
    now = [None, None]
    for plane in range(3, -1, -1):
        wait_rows(recv, 256, come_in.at[plane])
        rows = recv[256 * plane : 256 * plane + 256].astype(F32).reshape(8, 32, LANES)
        for ch in range(2):
            span = slice(64 * plane, 64 * plane + 64)
            signal[ch, span] = rows[:, 8 * ch : 8 * ch + 8].reshape(64, LANES)
            grad[ch, span] = rows[:, 8 * ch + 16 : 8 * ch + 24].reshape(64, LANES)
            build_shifted(ch, plane, grad, shifted)
        for ch in range(2):
            if plane == 3:
                now[ch] = turned(ch, 255, signal)
            last = 15 if plane == 3 else 4 * plane + 4
            for i in range(last, 4 * plane if plane else -1, -1):
                now[ch] = add_chunk(ch, i, signal, shifted, acc, now[ch])

    for ch in range(2):
        lags = regroup_lags(ch, acc, scale)
        send_c[:, 8 * ch : 8 * ch + 8, :] = lags.reshape(PEERS, 8, LANES)
    for peer in peers:
        pltpu.make_async_remote_copy(
            src_ref=send_c.at[peer],
            dst_ref=recv_c.at[me],
            send_sem=sent_c,
            recv_sem=come_c,
            device_id={"wide": peer},
            device_id_type=MESH,
        ).start()
    recv_c[me] = send_c[me]

    parts = []
    for ch in range(2):
        lags = send_c[:, 8 * ch : 8 * ch + 8, :].reshape(256, LANES)
        upper = lags.astype(BF16)
        parts += [upper, (lags - upper.astype(F32)).astype(BF16), upper]
    mixed = jnp.dot(
        jnp.concatenate(parts, axis=1),
        fine[...].reshape(6 * LANES, LANES),
        preferred_element_type=F32,
    )
    sums = jnp.sum(mixed * coarse[...], axis=0, keepdims=True)
    both = sums + pltpu.roll(sums, LANES - 16, 1)
    lane = lax.broadcasted_iota(jnp.int32, (1, LANES), 1)
    factor = jnp.where(lane < 64, factors[0], factors[1])
    line = jnp.where(lane % 64 < 16, scale * sums, factor * both)
    send_m[...] = line
    recv_m[me] = line

    for peer in peers:
        pltpu.make_async_remote_copy(
            src_ref=send_m,
            dst_ref=recv_m.at[me],
            send_sem=sent_m,
            recv_sem=come_m,
            device_id={"wide": peer},
            device_id_type=MESH,
        ).start()

    wait_rows(send, 32 * (PEERS - 1), sent_in)
    wait_rows(send_c, PEERS - 1, sent_c)
    wait_rows(recv_m, PEERS - 1, sent_m)
    wait_rows(recv_c, PEERS - 1, come_c)
    wait_rows(recv_m, PEERS - 1, come_m)


def regroup(c_ref, m_ref, out_ref, rg_ref, ld_ref):
    for ch in range(2):
        for k in range(8):
            out_ref[PEERS * ch : PEERS * (ch + 1), k * LANES : (k + 1) * LANES] = c_ref[
                :, 8 * ch + k, :
            ]
    lines = jnp.transpose(m_ref[:, 0, :])
    rg_ref[...] = jnp.concatenate([lines[0:16], lines[64:80]], axis=1)
    ld_ref[...] = jnp.concatenate([lines[16:32], lines[80:96]], axis=1)


def local(inputs, out_grad, residues, decay):
    chans, block = inputs.shape
    modes = residues.shape[1]
    vmem = pl.BlockSpec(memory_space=pltpu.VMEM)
    hbm = pl.BlockSpec(memory_space=pltpu.HBM)
    dma = pltpu.SemaphoreType.DMA
    lags, lines = pl.pallas_call(
        exchange,
        out_shape=(
            jax.ShapeDtypeStruct((PEERS, 16, LANES), F32),
            jax.ShapeDtypeStruct((PEERS, 1, LANES), F32),
        ),
        in_specs=[hbm] * 4,
        out_specs=(vmem, vmem),
        scratch_shapes=[
            pltpu.VMEM((chans, block), BF16),
            pltpu.VMEM((chans, block), BF16),
            pltpu.VMEM((modes, chans), F32),
            pltpu.VMEM((modes, chans), F32),
            pltpu.VMEM((1024, LANES), F32),
            pltpu.VMEM((1024, LANES), BF16),
            pltpu.VMEM((1024, LANES), BF16),
            pltpu.VMEM((2, 256, LANES), F32),
            pltpu.VMEM((2, 272, LANES), F32),
            pltpu.VMEM((2, 1024, 256), BF16),
            pltpu.VMEM((2, TURNS, 2, 264, LANES), F32),
            pltpu.VMEM((PEERS, 16, LANES), F32),
            pltpu.VMEM((2, 3, LANES, LANES), BF16),
            pltpu.VMEM((256, LANES), F32),
            pltpu.VMEM((1, LANES), F32),
            dma((4,)),
            dma,
            dma((4,)),
            dma,
            dma,
            dma,
            dma,
        ],
        compiler_params=pltpu.CompilerParams(
            collective_id=0, has_side_effects=True, vmem_limit_bytes=32 * 2**20
        ),
    )(*(pltpu.with_memory_space_constraint(a, pltpu.HBM) for a in (inputs, out_grad, residues.T, decay.T)))
    filter_grad, residue_grad, log_decay_grad = pl.pallas_call(
        regroup,
        out_shape=(
            jax.ShapeDtypeStruct((chans, block), F32),
            jax.ShapeDtypeStruct((modes, chans), F32),
            jax.ShapeDtypeStruct((modes, chans), F32),
        ),
        in_specs=[vmem] * 2,
        out_specs=(vmem,) * 3,
        compiler_params=pltpu.CompilerParams(vmem_limit_bytes=4 * 2**20),
    )(lags, lines)
    return filter_grad, residue_grad.T, log_decay_grad.T


def solution(mesh):
    placed = (P("narrow", "wide"), P("narrow", "wide"), P("narrow", None), P("narrow", None))
    return jax.shard_map(
        local,
        mesh=mesh,
        in_specs=placed,
        out_specs=(P("narrow", "wide"), P("narrow", None), P("narrow", None)),
        check_vma=False,
    )
```

```python
import math

import jax
import jax.numpy as jnp
from jax import lax
from jax.experimental import pallas as pl
from jax.experimental.pallas import tpu as pltpu
from jax.sharding import PartitionSpec as P

F32 = jnp.float32
BF16 = jnp.bfloat16
MESH = pl.DeviceIdType.MESH

LANES = 128
SHIFTS = 32
TURNS = LANES // SHIFTS
PEERS = 32
DISTANT = 10
RING = (0, 1, 2, 1)
OFFSETS = sorted(
    ((dz, dy, dc) for dz in range(4) for dy in range(4) for dc in range(2) if dz or dy or dc),
    key=lambda o: (-RING[o[0]] - RING[o[1]], -o[2], o),
)


def place(me):
    return me // 8, (me // 2) % 4, me % 2


def shifted_peer(at, dz, dy, dc):
    z, y, core = at
    return ((z + dz) % 4) * 8 + ((y + dy) % 4) * 2 + (core + dc) % 2


def aligned(index, size):
    return pl.ds(pl.multiple_of(index * size, size), size)


def to_rows(block_ref, which, stage):
    for ch in range(2):
        for k in range(8):
            stage[pl.ds(16 * which + 8 * ch + k, PEERS, stride=32), :] = block_ref[
                PEERS * ch : PEERS * (ch + 1), k * LANES : (k + 1) * LANES
            ].astype(F32)


def wait_rows(ref, rows, sem):
    part = ref.at[0:rows]
    pltpu.make_async_copy(part, part, sem).wait()


def turned(ch, m, signal):
    if m < 0:
        return jnp.zeros((SHIFTS, LANES), F32)
    spread = jnp.broadcast_to(signal[ch, pl.ds(m, 1), :], (SHIFTS, LANES))
    return pltpu.roll(spread, 0, 1, stride=1, stride_axis=0)


def toeplitz(ch, i, signal, now):
    row = lax.broadcasted_iota(jnp.int32, (SHIFTS, LANES), 0)
    lane = lax.broadcasted_iota(jnp.int32, (SHIFTS, LANES), 1)
    rows = []
    for m in range(16 * i + 15, 16 * i - 1, -1):
        before = turned(ch, m - 1, signal)
        rows.insert(0, jnp.where(lane >= row, now, before).astype(BF16))
        now = before
    halves = [jnp.concatenate(rows[:8], axis=0), jnp.concatenate(rows[8:], axis=0)]
    return jnp.concatenate(halves, axis=1), now


def build_shifted(ch, plane, grad, shifted):
    first = 64 * plane
    lane = lax.broadcasted_iota(jnp.int32, (72, LANES), 1)
    here = grad[ch, first : first + 72, :]
    after = grad[ch, first + 1 : first + 73, :]
    turns = []
    for h in range(TURNS):
        moved = here
        if h:
            moved = pltpu.roll(jnp.where(lane < SHIFTS * h, after, here), LANES - SHIFTS * h, 1)
        turns.append(jnp.concatenate([moved[0:64], moved[8:72]], axis=1).reshape(8, 8, 256))
    shifted[ch, 4 * first : 4 * first + 256] = (
        jnp.stack(turns, axis=1).reshape(256, 256).astype(BF16)
    )


def add_chunk(ch, i, signal, shifted, acc, now):
    live = 256 - 16 * i
    table, now = toeplitz(ch, i, signal, now)
    part = lax.dot_general(
        shifted[ch, 64 * i : 1024, :],
        table,
        (((1,), (1,)), ((), ())),
        preferred_element_type=F32,
    ).reshape(live // 8, TURNS, 8, 256)
    for h in range(TURNS):
        own = part[:, h].reshape(live, 256)
        for half in range(2):
            term = own[:, half * LANES : (half + 1) * LANES]
            if live > 16:
                acc[ch, h, half, 0 : live - 16] = acc[ch, h, half, 0 : live - 16] + term[: live - 16]
            acc[ch, h, half, live - 16 : live] = term[live - 16 :]
    return now


def regroup_lags(ch, acc, scale):
    group = lax.broadcasted_iota(jnp.int32, (256, LANES), 1) // SHIFTS
    total = None
    for turn in range(TURNS):
        mixed = None
        for low in range(TURNS):
            h = (low + turn) % TURNS
            term = acc[ch, h, 0, low : low + 256, :] + acc[ch, h, 1, low + 4 : low + 260, :]
            mixed = term if mixed is None else jnp.where(group == low, term, mixed)
        if turn:
            mixed = pltpu.roll(mixed, SHIFTS * turn, 1)
        total = mixed if total is None else total + mixed
    return total * scale


def channel_row(ref, channel):
    lane = lax.broadcasted_iota(jnp.int32, ref.shape, 1)
    column = jnp.sum(jnp.where(lane == channel, ref[...], 0.0), axis=1, keepdims=True)
    spread = jnp.broadcast_to(column, (16, LANES))
    sub = lax.broadcasted_iota(jnp.int32, (16, LANES), 0)
    lane = lax.broadcasted_iota(jnp.int32, (16, LANES), 1)
    return jnp.sum(jnp.where(lane % 16 == sub, spread, 0.0), axis=0, keepdims=True)


def exchange(
    x_hbm, g_hbm, res_hbm, dec_hbm, recv_c,
    x_ref, g_ref, res_ref, dec_ref, stage, send, recv, signal, grad, shifted,
    acc, send_c, fine, coarse,
    fetched, sent_in, come_in, sent_c, come_c,
):
    me = lax.axis_index("wide")
    at = place(me)
    peers = [shifted_peer(at, *offset) for offset in OFFSETS]
    scale = 1.0 / math.sqrt(PEERS * x_ref.shape[1])

    barrier = pltpu.get_barrier_semaphore()
    for peer in peers:
        pl.semaphore_signal(barrier, inc=1, device_id={"wide": peer}, device_id_type=MESH)

    fetches = [
        pltpu.make_async_copy(src, dst, fetched.at[n])
        for n, (src, dst) in enumerate(
            ((x_hbm, x_ref), (g_hbm, g_ref), (dec_hbm, dec_ref), (res_hbm, res_ref))
        )
    ]
    for fetch in fetches:
        fetch.start()
    for which, ref in enumerate((x_ref, g_ref)):
        fetches[which].wait()
        to_rows(ref, which, stage)
    send[...] = stage[...].astype(BF16)
    pl.semaphore_wait(barrier, PEERS - 1)

    for peer in peers:
        pltpu.make_async_remote_copy(
            src_ref=send.at[aligned(peer, 32), :],
            dst_ref=recv.at[aligned(me, 32), :],
            send_sem=sent_in,
            recv_sem=come_in.at[me // 8],
            device_id={"wide": peer},
            device_id_type=MESH,
        ).start()
    own = pltpu.make_async_copy(
        send.at[aligned(me, 32), :], recv.at[aligned(me, 32), :], come_in.at[me // 8]
    )
    own.start()

    fetches[2].wait()
    fetches[3].wait()
    lane_big = lax.broadcasted_iota(jnp.int32, (256, LANES), 1)
    block_at = (lax.broadcasted_iota(jnp.int32, (256, LANES), 0) * LANES).astype(F32)
    lane_small = lax.broadcasted_iota(jnp.int32, (LANES, LANES), 1)
    offset_at = lax.broadcasted_iota(jnp.int32, (LANES, LANES), 0).astype(F32)
    factors = []
    for ch in range(2):
        rate = channel_row(dec_ref, PEERS * ch + me)
        factors.append(-scale * rate * channel_row(res_ref, PEERS * ch + me))
        own = jnp.logical_and(lane_small >= 64 * ch, lane_small < 64 * ch + 48)
        power = jnp.where(own, jnp.exp(-rate * offset_at), 0.0)
        weighted = jnp.logical_and(lane_small % 64 >= 16, lane_small % 64 < 32)
        power = jnp.where(weighted, offset_at * power, power)
        upper = power.astype(BF16)
        fine[ch, 0] = upper
        fine[ch, 1] = upper
        fine[ch, 2] = (power - upper.astype(F32)).astype(BF16)
        power = jnp.exp(-rate * block_at)
        power = jnp.where(lane_big % 64 < 32, power, block_at * power)
        coarse[:, 64 * ch : 64 * ch + 64] = power[:, 64 * ch : 64 * ch + 64]

    grad[:, 256:] = jnp.zeros((2, 16, LANES), F32)
    acc[:, :, :, 256:] = jnp.zeros((2, TURNS, 2, 8, LANES), F32)
    now = [None, None]
    for plane in range(3, -1, -1):
        wait_rows(recv, 256, come_in.at[plane])
        rows = recv[256 * plane : 256 * plane + 256].astype(F32).reshape(8, 32, LANES)
        for ch in range(2):
            span = slice(64 * plane, 64 * plane + 64)
            signal[ch, span] = rows[:, 8 * ch : 8 * ch + 8].reshape(64, LANES)
            grad[ch, span] = rows[:, 8 * ch + 16 : 8 * ch + 24].reshape(64, LANES)
            build_shifted(ch, plane, grad, shifted)
        for ch in range(2):
            if plane == 3:
                now[ch] = turned(ch, 255, signal)
            last = 15 if plane == 3 else 4 * plane + 4
            for i in range(last, 4 * plane if plane else -1, -1):
                now[ch] = add_chunk(ch, i, signal, shifted, acc, now[ch])

    for ch in range(2):
        lags = regroup_lags(ch, acc, scale)
        send_c[:, 8 * ch : 8 * ch + 8, :] = lags.reshape(PEERS, 8, LANES)
    def reply(peer, rows):
        pltpu.make_async_remote_copy(
            src_ref=send_c.at[peer, rows, :],
            dst_ref=recv_c.at[me, rows, :],
            send_sem=sent_c,
            recv_sem=come_c,
            device_id={"wide": peer},
            device_id_type=MESH,
        ).start()

    for peer in peers[:DISTANT]:
        reply(peer, slice(0, 16))

    parts = []
    for ch in range(2):
        lags = send_c[:, 8 * ch : 8 * ch + 8, :].reshape(256, LANES)
        upper = lags.astype(BF16)
        parts += [upper, (lags - upper.astype(F32)).astype(BF16), upper]
    mixed = jnp.dot(
        jnp.concatenate(parts, axis=1),
        fine[...].reshape(6 * LANES, LANES),
        preferred_element_type=F32,
    )
    sums = jnp.sum(mixed * coarse[...], axis=0, keepdims=True)
    both = sums + pltpu.roll(sums, LANES - 16, 1)
    lane = lax.broadcasted_iota(jnp.int32, (1, LANES), 1)
    factor = jnp.where(lane < 64, factors[0], factors[1])
    line = jnp.where(lane % 64 < 16, scale * sums, factor * both)
    send_c[:, 16:17, :] = jnp.broadcast_to(line[None], (PEERS, 1, LANES))
    for peer in peers[:DISTANT]:
        reply(peer, slice(16, 17))
    for peer in peers[DISTANT:]:
        reply(peer, slice(0, 17))
    recv_c[me] = send_c[me]

    wait_rows(send, 32 * (PEERS - 1), sent_in)
    part = send_c.at[0 : PEERS - 1, 0:17, :]
    pltpu.make_async_copy(part, part, sent_c).wait()
    pltpu.make_async_copy(part, part, come_c).wait()


def regroup(c_ref, out_ref, rg_ref, ld_ref):
    for ch in range(2):
        for k in range(8):
            out_ref[PEERS * ch : PEERS * (ch + 1), k * LANES : (k + 1) * LANES] = c_ref[
                :, 8 * ch + k, :
            ]
    lines = jnp.transpose(c_ref[:, 16, :])
    rg_ref[...] = jnp.concatenate([lines[0:16], lines[64:80]], axis=1)
    ld_ref[...] = jnp.concatenate([lines[16:32], lines[80:96]], axis=1)


def local(inputs, out_grad, residues, decay):
    chans, block = inputs.shape
    modes = residues.shape[1]
    vmem = pl.BlockSpec(memory_space=pltpu.VMEM)
    hbm = pl.BlockSpec(memory_space=pltpu.HBM)
    dma = pltpu.SemaphoreType.DMA
    replies = pl.pallas_call(
        exchange,
        out_shape=jax.ShapeDtypeStruct((PEERS, 24, LANES), F32),
        in_specs=[hbm] * 4,
        out_specs=vmem,
        scratch_shapes=[
            pltpu.VMEM((chans, block), BF16),
            pltpu.VMEM((chans, block), BF16),
            pltpu.VMEM((modes, chans), F32),
            pltpu.VMEM((modes, chans), F32),
            pltpu.VMEM((1024, LANES), F32),
            pltpu.VMEM((1024, LANES), BF16),
            pltpu.VMEM((1024, LANES), BF16),
            pltpu.VMEM((2, 256, LANES), F32),
            pltpu.VMEM((2, 272, LANES), F32),
            pltpu.VMEM((2, 1024, 256), BF16),
            pltpu.VMEM((2, TURNS, 2, 264, LANES), F32),
            pltpu.VMEM((PEERS, 24, LANES), F32),
            pltpu.VMEM((2, 3, LANES, LANES), BF16),
            pltpu.VMEM((256, LANES), F32),
            dma((4,)),
            dma,
            dma((4,)),
            dma,
            dma,
        ],
        compiler_params=pltpu.CompilerParams(
            collective_id=0, has_side_effects=True, vmem_limit_bytes=32 * 2**20
        ),
    )(*(pltpu.with_memory_space_constraint(a, pltpu.HBM) for a in (inputs, out_grad, residues.T, decay.T)))
    filter_grad, residue_grad, log_decay_grad = pl.pallas_call(
        regroup,
        out_shape=(
            jax.ShapeDtypeStruct((chans, block), F32),
            jax.ShapeDtypeStruct((modes, chans), F32),
            jax.ShapeDtypeStruct((modes, chans), F32),
        ),
        in_specs=[vmem],
        out_specs=(vmem,) * 3,
        compiler_params=pltpu.CompilerParams(vmem_limit_bytes=4 * 2**20),
    )(replies)
    return filter_grad, residue_grad.T, log_decay_grad.T


def solution(mesh):
    placed = (P("narrow", "wide"), P("narrow", "wide"), P("narrow", None), P("narrow", None))
    return jax.shard_map(
        local,
        mesh=mesh,
        in_specs=placed,
        out_specs=(P("narrow", "wide"), P("narrow", None), P("narrow", None)),
        check_vma=False,
    )
```

```python
import math

import jax
import jax.numpy as jnp
from jax import lax
from jax.experimental import pallas as pl
from jax.experimental.pallas import tpu as pltpu
from jax.sharding import PartitionSpec as P

F32 = jnp.float32
BF16 = jnp.bfloat16
PAIRS = ((0, 0), (0, 1), (1, 0), (1, 1), (0, 2), (2, 0))
MESH = pl.DeviceIdType.MESH

LANES = 128
SHIFTS = 32
TURNS = LANES // SHIFTS
PEERS = 32
GROUPS = ((24, 8), (16, 8), (12, 4), (0, 12))
DISTANT = 10
RING = (0, 1, 2, 1)
OFFSETS = sorted(
    ((dz, dy, dc) for dz in range(4) for dy in range(4) for dc in range(2) if dz or dy or dc),
    key=lambda o: (-RING[o[0]] - RING[o[1]], -o[2], o),
)


def place(me):
    return me // 8, (me // 2) % 4, me % 2


def shifted_peer(at, dz, dy, dc):
    z, y, core = at
    return ((z + dz) % 4) * 8 + ((y + dy) % 4) * 2 + (core + dc) % 2


def aligned(index, size):
    return pl.ds(pl.multiple_of(index * size, size), size)


def to_rows(block_ref, which, stage):
    for ch in range(2):
        for k in range(8):
            stage[pl.ds(16 * which + 8 * ch + k, PEERS, stride=32), :] = block_ref[
                PEERS * ch : PEERS * (ch + 1), k * LANES : (k + 1) * LANES
            ].astype(F32)


def wait_rows(ref, rows, sem):
    part = ref.at[0:rows]
    pltpu.make_async_copy(part, part, sem).wait()


def turned(ch, m, signal):
    if m < 0:
        return jnp.zeros((SHIFTS, LANES), F32)
    spread = jnp.broadcast_to(signal[ch, pl.ds(m, 1), :], (SHIFTS, LANES))
    return pltpu.roll(spread, 0, 1, stride=1, stride_axis=0)


def toeplitz(ch, i, signal, now):
    row = lax.broadcasted_iota(jnp.int32, (SHIFTS, LANES), 0)
    lane = lax.broadcasted_iota(jnp.int32, (SHIFTS, LANES), 1)
    rows = []
    for m in range(16 * i + 15, 16 * i - 1, -1):
        before = turned(ch, m - 1, signal)
        rows.insert(0, jnp.where(lane >= row, now, before).astype(BF16))
        now = before
    halves = [jnp.concatenate(rows[:8], axis=0), jnp.concatenate(rows[8:], axis=0)]
    return jnp.concatenate(halves, axis=1), now


def build_shifted(ch, first, count, grad, shifted):
    lane = lax.broadcasted_iota(jnp.int32, (count + 8, LANES), 1)
    here = grad[ch, first : first + count + 8, :]
    after = grad[ch, first + 1 : first + count + 9, :]
    turns = []
    for h in range(TURNS):
        moved = here
        if h:
            moved = pltpu.roll(jnp.where(lane < SHIFTS * h, after, here), LANES - SHIFTS * h, 1)
        both = jnp.concatenate([moved[0:count], moved[8 : count + 8]], axis=1)
        turns.append(both.reshape(count // 8, 8, 256))
    shifted[ch, 4 * first : 4 * first + 4 * count] = (
        jnp.stack(turns, axis=1).reshape(4 * count, 256).astype(BF16)
    )


def add_chunk(ch, i, signal, shifted, acc, now):
    live = 256 - 16 * i
    table, now = toeplitz(ch, i, signal, now)
    part = lax.dot_general(
        shifted[ch, 64 * i : 1024, :],
        table,
        (((1,), (1,)), ((), ())),
        preferred_element_type=F32,
    ).reshape(live // 8, TURNS, 8, 256)
    for h in range(TURNS):
        own = part[:, h].reshape(live, 256)
        for half in range(2):
            term = own[:, half * LANES : (half + 1) * LANES]
            if live > 16:
                acc[ch, h, half, 0 : live - 16] = acc[ch, h, half, 0 : live - 16] + term[: live - 16]
            acc[ch, h, half, live - 16 : live] = term[live - 16 :]
    return now


def regroup_lags(ch, acc, scale):
    group = lax.broadcasted_iota(jnp.int32, (256, LANES), 1) // SHIFTS
    total = None
    for turn in range(TURNS):
        mixed = None
        for low in range(TURNS):
            h = (low + turn) % TURNS
            term = acc[ch, h, 0, low : low + 256, :] + acc[ch, h, 1, low + 4 : low + 260, :]
            mixed = term if mixed is None else jnp.where(group == low, term, mixed)
        if turn:
            mixed = pltpu.roll(mixed, SHIFTS * turn, 1)
        total = mixed if total is None else total + mixed
    return total * scale


def channel_row(ref, channel):
    lane = lax.broadcasted_iota(jnp.int32, ref.shape, 1)
    column = jnp.sum(jnp.where(lane == channel, ref[...], 0.0), axis=1, keepdims=True)
    spread = jnp.broadcast_to(column, (16, LANES))
    sub = lax.broadcasted_iota(jnp.int32, (16, LANES), 0)
    lane = lax.broadcasted_iota(jnp.int32, (16, LANES), 1)
    return jnp.sum(jnp.where(lane % 16 == sub, spread, 0.0), axis=0, keepdims=True)


def split(values):
    parts = []
    for _ in range(3):
        part = values.astype(BF16)
        parts.append(part)
        values = values - part.astype(F32)
    return parts


def exchange(
    x_hbm, g_hbm, res_hbm, dec_hbm, recv_c,
    x_ref, g_ref, res_ref, dec_ref, stage, send, recv, signal, grad, shifted,
    acc, send_c, fine, coarse,
    fetched, sent_in, come_in, sent_c, come_c,
):
    me = lax.axis_index("wide")
    at = place(me)
    peers = [shifted_peer(at, *offset) for offset in OFFSETS]
    scale = 1.0 / math.sqrt(PEERS * x_ref.shape[1])

    barrier = pltpu.get_barrier_semaphore()
    for peer in peers:
        pl.semaphore_signal(barrier, inc=1, device_id={"wide": peer}, device_id_type=MESH)

    fetches = [
        pltpu.make_async_copy(src, dst, fetched.at[n])
        for n, (src, dst) in enumerate(
            ((x_hbm, x_ref), (g_hbm, g_ref), (dec_hbm, dec_ref), (res_hbm, res_ref))
        )
    ]
    for fetch in fetches:
        fetch.start()
    for which, ref in enumerate((x_ref, g_ref)):
        fetches[which].wait()
        to_rows(ref, which, stage)
    send[...] = stage[...].astype(BF16)
    pl.semaphore_wait(barrier, PEERS - 1)

    group = len(GROUPS) - 1
    for n in range(len(GROUPS) - 2, -1, -1):
        group = jnp.where(me >= GROUPS[n][0], n, group)
    for peer in peers:
        pltpu.make_async_remote_copy(
            src_ref=send.at[aligned(peer, 32), :],
            dst_ref=recv.at[aligned(me, 32), :],
            send_sem=sent_in,
            recv_sem=come_in.at[group],
            device_id={"wide": peer},
            device_id_type=MESH,
        ).start()
    own = pltpu.make_async_copy(
        send.at[aligned(me, 32), :], recv.at[aligned(me, 32), :], come_in.at[group]
    )
    own.start()

    fetches[2].wait()
    fetches[3].wait()
    lane_big = lax.broadcasted_iota(jnp.int32, (256, LANES), 1)
    block_at = (lax.broadcasted_iota(jnp.int32, (256, LANES), 0) * LANES).astype(F32)
    lane_small = lax.broadcasted_iota(jnp.int32, (LANES, LANES), 1)
    offset_at = lax.broadcasted_iota(jnp.int32, (LANES, LANES), 0).astype(F32)
    factors = []
    for ch in range(2):
        rate = channel_row(dec_ref, PEERS * ch + me)
        factors.append(-scale * rate * channel_row(res_ref, PEERS * ch + me))
        own = jnp.logical_and(lane_small >= 64 * ch, lane_small < 64 * ch + 48)
        power = jnp.where(own, jnp.exp(-rate * offset_at), 0.0)
        weighted = jnp.logical_and(lane_small % 64 >= 16, lane_small % 64 < 32)
        power = jnp.where(weighted, offset_at * power, power)
        thirds = split(power)
        for n, (_, which) in enumerate(PAIRS):
            fine[ch, n] = thirds[which]
        power = jnp.exp(-rate * block_at)
        power = jnp.where(lane_big % 64 < 32, power, block_at * power)
        coarse[:, 64 * ch : 64 * ch + 64] = power[:, 64 * ch : 64 * ch + 64]

    grad[:, 256:] = jnp.zeros((2, 16, LANES), F32)
    acc[:, :, :, 256:] = jnp.zeros((2, TURNS, 2, 8, LANES), F32)
    now = [None, None]
    last = 15
    for n, (first, count) in enumerate(GROUPS):
        wait_rows(recv, 32 * count, come_in.at[n])
        rows = recv[32 * first : 32 * (first + count)].astype(F32).reshape(count, 32, LANES)
        for ch in range(2):
            span = slice(8 * first, 8 * (first + count))
            signal[ch, span] = rows[:, 8 * ch : 8 * ch + 8].reshape(8 * count, LANES)
            grad[ch, span] = rows[:, 8 * ch + 16 : 8 * ch + 24].reshape(8 * count, LANES)
        least = first // 2 + 1 if first else 0
        for ch in range(2):
            if n == 0:
                now[ch] = turned(ch, 255, signal)
            else:
                now[ch] = add_chunk(ch, last, signal, shifted, acc, now[ch])
        for ch in range(2):
            build_shifted(ch, 8 * first, 8 * count, grad, shifted)
        if n:
            last -= 1
        for ch in range(2):
            for i in range(last, least - 1, -1):
                now[ch] = add_chunk(ch, i, signal, shifted, acc, now[ch])
            if first == 0:
                lags = regroup_lags(ch, acc, scale)
                send_c[:, 8 * ch : 8 * ch + 8, :] = lags.reshape(PEERS, 8, LANES)
        last = least - 1

    def reply(peer, rows):
        pltpu.make_async_remote_copy(
            src_ref=send_c.at[peer, rows, :],
            dst_ref=recv_c.at[me, rows, :],
            send_sem=sent_c,
            recv_sem=come_c,
            device_id={"wide": peer},
            device_id_type=MESH,
        ).start()

    for peer in peers[:DISTANT]:
        reply(peer, slice(0, 16))

    parts = []
    for ch in range(2):
        lags = send_c[:, 8 * ch : 8 * ch + 8, :].reshape(256, LANES)
        thirds = split(lags)
        parts += [thirds[which] for which, _ in PAIRS]
    mixed = jnp.dot(
        jnp.concatenate(parts, axis=1),
        fine[...].reshape(2 * len(PAIRS) * LANES, LANES),
        preferred_element_type=F32,
    )
    sums = jnp.sum(mixed * coarse[...], axis=0, keepdims=True)
    both = sums + pltpu.roll(sums, LANES - 16, 1)
    lane = lax.broadcasted_iota(jnp.int32, (1, LANES), 1)
    factor = jnp.where(lane < 64, factors[0], factors[1])
    line = jnp.where(lane % 64 < 16, scale * sums, factor * both)
    send_c[:, 16:17, :] = jnp.broadcast_to(line[None], (PEERS, 1, LANES))
    for peer in peers[:DISTANT]:
        reply(peer, slice(16, 17))
    for peer in peers[DISTANT:]:
        reply(peer, slice(0, 17))
    recv_c[me, 0:17] = send_c[me, 0:17]

    wait_rows(send, 32 * (PEERS - 1), sent_in)
    part = send_c.at[0 : PEERS - 1, 0:17, :]
    pltpu.make_async_copy(part, part, sent_c).wait()
    pltpu.make_async_copy(part, part, come_c).wait()


def regroup(c_ref, out_ref, rg_ref, ld_ref):
    for ch in range(2):
        for k in range(8):
            out_ref[PEERS * ch : PEERS * (ch + 1), k * LANES : (k + 1) * LANES] = c_ref[
                :, 8 * ch + k, :
            ]
    lines = jnp.transpose(c_ref[:, 16, :])
    rg_ref[...] = jnp.concatenate([lines[0:16], lines[64:80]], axis=1)
    ld_ref[...] = jnp.concatenate([lines[16:32], lines[80:96]], axis=1)


def local(inputs, out_grad, residues, decay):
    chans, block = inputs.shape
    modes = residues.shape[1]
    vmem = pl.BlockSpec(memory_space=pltpu.VMEM)
    hbm = pl.BlockSpec(memory_space=pltpu.HBM)
    dma = pltpu.SemaphoreType.DMA
    replies = pl.pallas_call(
        exchange,
        out_shape=jax.ShapeDtypeStruct((PEERS, 24, LANES), F32),
        in_specs=[hbm] * 4,
        out_specs=vmem,
        scratch_shapes=[
            pltpu.VMEM((chans, block), BF16),
            pltpu.VMEM((chans, block), BF16),
            pltpu.VMEM((modes, chans), F32),
            pltpu.VMEM((modes, chans), F32),
            pltpu.VMEM((1024, LANES), F32),
            pltpu.VMEM((1024, LANES), BF16),
            pltpu.VMEM((1024, LANES), BF16),
            pltpu.VMEM((2, 256, LANES), F32),
            pltpu.VMEM((2, 272, LANES), F32),
            pltpu.VMEM((2, 1024, 256), BF16),
            pltpu.VMEM((2, TURNS, 2, 264, LANES), F32),
            pltpu.VMEM((PEERS, 24, LANES), F32),
            pltpu.VMEM((2, len(PAIRS), LANES, LANES), BF16),
            pltpu.VMEM((256, LANES), F32),
            dma((4,)),
            dma,
            dma((len(GROUPS),)),
            dma,
            dma,
        ],
        compiler_params=pltpu.CompilerParams(
            collective_id=0, has_side_effects=True, vmem_limit_bytes=32 * 2**20
        ),
    )(*(pltpu.with_memory_space_constraint(a, pltpu.HBM) for a in (inputs, out_grad, residues.T, decay.T)))
    filter_grad, residue_grad, log_decay_grad = pl.pallas_call(
        regroup,
        out_shape=(
            jax.ShapeDtypeStruct((chans, block), F32),
            jax.ShapeDtypeStruct((modes, chans), F32),
            jax.ShapeDtypeStruct((modes, chans), F32),
        ),
        in_specs=[vmem],
        out_specs=(vmem,) * 3,
        compiler_params=pltpu.CompilerParams(vmem_limit_bytes=4 * 2**20),
    )(replies)
    return filter_grad, residue_grad.T, log_decay_grad.T


def solution(mesh):
    placed = (P("narrow", "wide"), P("narrow", "wide"), P("narrow", None), P("narrow", None))
    return jax.shard_map(
        local,
        mesh=mesh,
        in_specs=placed,
        out_specs=(P("narrow", "wide"), P("narrow", None), P("narrow", None)),
        check_vma=False,
    )
```

```python
import math

import jax
import jax.numpy as jnp
from jax import lax
from jax.experimental import pallas as pl
from jax.experimental.pallas import tpu as pltpu
from jax.sharding import PartitionSpec as P

F32 = jnp.float32
BF16 = jnp.bfloat16
PAIRS = ((0, 0), (0, 1), (1, 0), (1, 1), (0, 2), (2, 0))
MESH = pl.DeviceIdType.MESH

LANES = 128
SHIFTS = 32
TURNS = LANES // SHIFTS
PEERS = 32
GROUPS = ((24, 8), (16, 8), (12, 4), (0, 12))
DISTANT = 10
RING = (0, 1, 2, 1)
OFFSETS = sorted(
    ((dz, dy, dc) for dz in range(4) for dy in range(4) for dc in range(2) if dz or dy or dc),
    key=lambda o: (-RING[o[0]] - RING[o[1]], -o[2], o),
)


def place(me):
    return me // 8, (me // 2) % 4, me % 2


def shifted_peer(at, dz, dy, dc):
    z, y, core = at
    return ((z + dz) % 4) * 8 + ((y + dy) % 4) * 2 + (core + dc) % 2


def aligned(index, size):
    return pl.ds(pl.multiple_of(index * size, size), size)


def to_rows(block_ref, which, stage):
    for ch in range(2):
        for k in range(8):
            stage[pl.ds(16 * which + 8 * ch + k, PEERS, stride=32), :] = block_ref[
                PEERS * ch : PEERS * (ch + 1), k * LANES : (k + 1) * LANES
            ].astype(F32)


def wait_rows(ref, rows, sem):
    part = ref.at[0:rows]
    pltpu.make_async_copy(part, part, sem).wait()


def turned(ch, m, signal):
    if m < 0:
        return jnp.zeros((SHIFTS, LANES), F32)
    spread = jnp.broadcast_to(signal[ch, pl.ds(m, 1), :], (SHIFTS, LANES))
    return pltpu.roll(spread, 0, 1, stride=1, stride_axis=0)


def toeplitz(ch, i, signal, now):
    row = lax.broadcasted_iota(jnp.int32, (SHIFTS, LANES), 0)
    lane = lax.broadcasted_iota(jnp.int32, (SHIFTS, LANES), 1)
    rows = []
    for m in range(16 * i + 15, 16 * i - 1, -1):
        before = turned(ch, m - 1, signal)
        rows.insert(0, jnp.where(lane >= row, now, before).astype(BF16))
        now = before
    halves = [jnp.concatenate(rows[:8], axis=0), jnp.concatenate(rows[8:], axis=0)]
    return jnp.concatenate(halves, axis=1), now


def build_shifted(ch, first, count, grad, shifted):
    lane = lax.broadcasted_iota(jnp.int32, (count + 8, LANES), 1)
    here = grad[ch, first : first + count + 8, :]
    after = grad[ch, first + 1 : first + count + 9, :]
    turns = []
    for h in range(TURNS):
        moved = here
        if h:
            moved = pltpu.roll(jnp.where(lane < SHIFTS * h, after, here), LANES - SHIFTS * h, 1)
        both = jnp.concatenate([moved[0:count], moved[8 : count + 8]], axis=1)
        turns.append(both.reshape(count // 8, 8, 256))
    shifted[ch, 4 * first : 4 * first + 4 * count] = (
        jnp.stack(turns, axis=1).reshape(4 * count, 256).astype(BF16)
    )


def add_chunk(ch, i, signal, shifted, acc, now):
    live = 256 - 16 * i
    table, now = toeplitz(ch, i, signal, now)
    part = lax.dot_general(
        shifted[ch, 64 * i : 1024, :],
        table,
        (((1,), (1,)), ((), ())),
        preferred_element_type=F32,
    ).reshape(live // 8, TURNS, 8, 256)
    for h in range(TURNS):
        own = part[:, h].reshape(live, 256)
        for half in range(2):
            term = own[:, half * LANES : (half + 1) * LANES]
            if live > 16:
                acc[ch, h, half, 0 : live - 16] = acc[ch, h, half, 0 : live - 16] + term[: live - 16]
            acc[ch, h, half, live - 16 : live] = term[live - 16 :]
    return now


def regroup_lags(ch, acc, scale):
    group = lax.broadcasted_iota(jnp.int32, (256, LANES), 1) // SHIFTS
    total = None
    for turn in range(TURNS):
        mixed = None
        for low in range(TURNS):
            h = (low + turn) % TURNS
            term = acc[ch, h, 0, low : low + 256, :] + acc[ch, h, 1, low + 4 : low + 260, :]
            mixed = term if mixed is None else jnp.where(group == low, term, mixed)
        if turn:
            mixed = pltpu.roll(mixed, SHIFTS * turn, 1)
        total = mixed if total is None else total + mixed
    return total * scale


def channel_row(ref, channel):
    lane = lax.broadcasted_iota(jnp.int32, ref.shape, 1)
    column = jnp.sum(jnp.where(lane == channel, ref[...], 0.0), axis=1, keepdims=True)
    spread = jnp.broadcast_to(column, (16, LANES))
    sub = lax.broadcasted_iota(jnp.int32, (16, LANES), 0)
    lane = lax.broadcasted_iota(jnp.int32, (16, LANES), 1)
    return jnp.sum(jnp.where(lane % 16 == sub, spread, 0.0), axis=0, keepdims=True)


def split(values):
    parts = []
    for _ in range(3):
        part = values.astype(BF16)
        parts.append(part)
        values = values - part.astype(F32)
    return parts


def exchange(
    x_hbm, g_hbm, res_hbm, dec_hbm, lags_ref, lines_ref, recv_c,
    x_ref, g_ref, res_ref, dec_ref, stage, send, recv, signal, grad, shifted,
    acc, send_c, fine, coarse,
    fetched, sent_in, come_in, sent_c, come_c,
):
    me = lax.axis_index("wide")
    at = place(me)
    peers = [shifted_peer(at, *offset) for offset in OFFSETS]
    scale = 1.0 / math.sqrt(PEERS * x_ref.shape[1])

    barrier = pltpu.get_barrier_semaphore()
    for peer in peers:
        pl.semaphore_signal(barrier, inc=1, device_id={"wide": peer}, device_id_type=MESH)

    fetches = [
        pltpu.make_async_copy(src, dst, fetched.at[n])
        for n, (src, dst) in enumerate(
            ((x_hbm, x_ref), (g_hbm, g_ref), (dec_hbm, dec_ref), (res_hbm, res_ref))
        )
    ]
    for fetch in fetches:
        fetch.start()
    for which, ref in enumerate((x_ref, g_ref)):
        fetches[which].wait()
        to_rows(ref, which, stage)
    send[...] = stage[...].astype(BF16)
    pl.semaphore_wait(barrier, PEERS - 1)

    group = len(GROUPS) - 1
    for n in range(len(GROUPS) - 2, -1, -1):
        group = jnp.where(me >= GROUPS[n][0], n, group)
    for peer in peers:
        pltpu.make_async_remote_copy(
            src_ref=send.at[aligned(peer, 32), :],
            dst_ref=recv.at[aligned(me, 32), :],
            send_sem=sent_in,
            recv_sem=come_in.at[group],
            device_id={"wide": peer},
            device_id_type=MESH,
        ).start()
    own = pltpu.make_async_copy(
        send.at[aligned(me, 32), :], recv.at[aligned(me, 32), :], come_in.at[group]
    )
    own.start()

    fetches[2].wait()
    fetches[3].wait()
    lane_big = lax.broadcasted_iota(jnp.int32, (256, LANES), 1)
    block_at = (lax.broadcasted_iota(jnp.int32, (256, LANES), 0) * LANES).astype(F32)
    lane_small = lax.broadcasted_iota(jnp.int32, (LANES, LANES), 1)
    offset_at = lax.broadcasted_iota(jnp.int32, (LANES, LANES), 0).astype(F32)
    factors = []
    for ch in range(2):
        rate = channel_row(dec_ref, PEERS * ch + me)
        factors.append(-scale * rate * channel_row(res_ref, PEERS * ch + me))
        own = jnp.logical_and(lane_small >= 64 * ch, lane_small < 64 * ch + 48)
        power = jnp.where(own, jnp.exp(-rate * offset_at), 0.0)
        weighted = jnp.logical_and(lane_small % 64 >= 16, lane_small % 64 < 32)
        power = jnp.where(weighted, offset_at * power, power)
        thirds = split(power)
        for n, (_, which) in enumerate(PAIRS):
            fine[ch, n] = thirds[which]
        power = jnp.exp(-rate * block_at)
        power = jnp.where(lane_big % 64 < 32, power, block_at * power)
        coarse[:, 64 * ch : 64 * ch + 64] = power[:, 64 * ch : 64 * ch + 64]

    grad[:, 256:] = jnp.zeros((2, 16, LANES), F32)
    acc[:, :, :, 256:] = jnp.zeros((2, TURNS, 2, 8, LANES), F32)
    now = [None, None]
    last = 15
    for n, (first, count) in enumerate(GROUPS):
        wait_rows(recv, 32 * count, come_in.at[n])
        rows = recv[32 * first : 32 * (first + count)].astype(F32).reshape(count, 32, LANES)
        for ch in range(2):
            span = slice(8 * first, 8 * (first + count))
            signal[ch, span] = rows[:, 8 * ch : 8 * ch + 8].reshape(8 * count, LANES)
            grad[ch, span] = rows[:, 8 * ch + 16 : 8 * ch + 24].reshape(8 * count, LANES)
        least = first // 2 + 1 if first else 0
        for ch in range(2):
            if n == 0:
                now[ch] = turned(ch, 255, signal)
            else:
                now[ch] = add_chunk(ch, last, signal, shifted, acc, now[ch])
        for ch in range(2):
            build_shifted(ch, 8 * first, 8 * count, grad, shifted)
        if n:
            last -= 1
        for ch in range(2):
            for i in range(last, least - 1, -1):
                now[ch] = add_chunk(ch, i, signal, shifted, acc, now[ch])
            if first == 0:
                lags = regroup_lags(ch, acc, scale)
                send_c[:, 8 * ch : 8 * ch + 8, :] = lags.reshape(PEERS, 8, LANES)
        last = least - 1

    def reply(peer, rows):
        pltpu.make_async_remote_copy(
            src_ref=send_c.at[peer, rows, :],
            dst_ref=recv_c.at[me, rows, :],
            send_sem=sent_c,
            recv_sem=come_c.at[me // 8],
            device_id={"wide": peer},
            device_id_type=MESH,
        ).start()

    for peer in peers[:DISTANT]:
        reply(peer, slice(0, 16))

    parts = []
    for ch in range(2):
        lags = send_c[:, 8 * ch : 8 * ch + 8, :].reshape(256, LANES)
        thirds = split(lags)
        parts += [thirds[which] for which, _ in PAIRS]
    mixed = jnp.dot(
        jnp.concatenate(parts, axis=1),
        fine[...].reshape(2 * len(PAIRS) * LANES, LANES),
        preferred_element_type=F32,
    )
    sums = jnp.sum(mixed * coarse[...], axis=0, keepdims=True)
    both = sums + pltpu.roll(sums, LANES - 16, 1)
    lane = lax.broadcasted_iota(jnp.int32, (1, LANES), 1)
    factor = jnp.where(lane < 64, factors[0], factors[1])
    line = jnp.where(lane % 64 < 16, scale * sums, factor * both)
    send_c[:, 16:17, :] = jnp.broadcast_to(line[None], (PEERS, 1, LANES))
    for peer in peers[:DISTANT]:
        reply(peer, slice(16, 17))
    for peer in peers[DISTANT:]:
        reply(peer, slice(0, 17))
    own = pltpu.make_async_copy(
        send_c.at[me, 0:17, :], recv_c.at[me, 0:17, :], come_c.at[me // 8]
    )
    own.start()

    wait_rows(send, 32 * (PEERS - 1), sent_in)
    part = send_c.at[0 : PEERS - 1, 0:17, :]
    pltpu.make_async_copy(part, part, sent_c).wait()
    for plane in range(3, -1, -1):
        part = recv_c.at[8 * plane : 8 * plane + 8, 0:17, :]
        pltpu.make_async_copy(part, part, come_c.at[plane]).wait()
        for ch in range(2):
            for k in range(8):
                lags_ref[
                    PEERS * ch + 8 * plane : PEERS * ch + 8 * plane + 8,
                    k * LANES : (k + 1) * LANES,
                ] = recv_c[8 * plane : 8 * plane + 8, 8 * ch + k, :]
        lines_ref[8 * plane : 8 * plane + 8, :] = recv_c[8 * plane : 8 * plane + 8, 16, :]


def regroup(lags_ref, lines_ref, out_hbm, rg_hbm, ld_hbm, rg_ref, ld_ref, sems):
    copies = [
        pltpu.make_async_copy(src, dst, sems.at[n])
        for n, (src, dst) in enumerate(((lags_ref, out_hbm), (rg_ref, rg_hbm), (ld_ref, ld_hbm)))
    ]
    copies[0].start()
    lines = jnp.transpose(lines_ref[...])
    rg_ref[...] = jnp.concatenate([lines[0:16], lines[64:80]], axis=1)
    copies[1].start()
    ld_ref[...] = jnp.concatenate([lines[16:32], lines[80:96]], axis=1)
    copies[2].start()
    for copy in copies:
        copy.wait()


def local(inputs, out_grad, residues, decay):
    chans, block = inputs.shape
    modes = residues.shape[1]
    vmem = pl.BlockSpec(memory_space=pltpu.VMEM)
    hbm = pl.BlockSpec(memory_space=pltpu.HBM)
    dma = pltpu.SemaphoreType.DMA
    lags, lines = pl.pallas_call(
        exchange,
        out_shape=(
            jax.ShapeDtypeStruct((chans, block), F32),
            jax.ShapeDtypeStruct((PEERS, LANES), F32),
        ),
        in_specs=[hbm] * 4,
        out_specs=(vmem, vmem),
        scratch_shapes=[
            pltpu.VMEM((PEERS, 24, LANES), F32),
            pltpu.VMEM((chans, block), BF16),
            pltpu.VMEM((chans, block), BF16),
            pltpu.VMEM((modes, chans), F32),
            pltpu.VMEM((modes, chans), F32),
            pltpu.VMEM((1024, LANES), F32),
            pltpu.VMEM((1024, LANES), BF16),
            pltpu.VMEM((1024, LANES), BF16),
            pltpu.VMEM((2, 256, LANES), F32),
            pltpu.VMEM((2, 272, LANES), F32),
            pltpu.VMEM((2, 1024, 256), BF16),
            pltpu.VMEM((2, TURNS, 2, 264, LANES), F32),
            pltpu.VMEM((PEERS, 24, LANES), F32),
            pltpu.VMEM((2, len(PAIRS), LANES, LANES), BF16),
            pltpu.VMEM((256, LANES), F32),
            dma((4,)),
            dma,
            dma((len(GROUPS),)),
            dma,
            dma((4,)),
        ],
        compiler_params=pltpu.CompilerParams(
            collective_id=0, has_side_effects=True, vmem_limit_bytes=32 * 2**20
        ),
    )(*(pltpu.with_memory_space_constraint(a, pltpu.HBM) for a in (inputs, out_grad, residues.T, decay.T)))
    filter_grad, residue_grad, log_decay_grad = pl.pallas_call(
        regroup,
        out_shape=(
            jax.ShapeDtypeStruct((chans, block), F32),
            jax.ShapeDtypeStruct((modes, chans), F32),
            jax.ShapeDtypeStruct((modes, chans), F32),
        ),
        in_specs=[vmem] * 2,
        out_specs=(hbm,) * 3,
        scratch_shapes=[
            pltpu.VMEM((modes, chans), F32),
            pltpu.VMEM((modes, chans), F32),
            dma((3,)),
        ],
        compiler_params=pltpu.CompilerParams(vmem_limit_bytes=4 * 2**20),
    )(lags, lines)
    return filter_grad, residue_grad.T, log_decay_grad.T


def solution(mesh):
    placed = (P("narrow", "wide"), P("narrow", "wide"), P("narrow", None), P("narrow", None))
    return jax.shard_map(
        local,
        mesh=mesh,
        in_specs=placed,
        out_specs=(P("narrow", "wide"), P("narrow", None), P("narrow", None)),
        check_vma=False,
    )
```
